32 devices in a mesh: row: 8 (over y, x, core), col: 4 (over z).
Axes of the slice: x: 2, y: 2, z: 4, core: 2. Of those that a mesh axis runs over, the one named last changes fastest.
Arguments:
- covariance: float32 [3, 8, 6, 4, 128, 128], P(None, 'row', None, 'col'), may hold values from -2 to 2, as said below
- tile_mask: int32 [24, 24], replicated, may hold values from 0 to 1, as said below
Outputs:
- updated: bfloat16 [3, 8, 6, 4, 128, 128], P(None, 'row', None, 'col')
The draws below stay inside these ranges and needn't reach their ends.
Inputs may be any that keep to these rules, and one draw needn't show every extreme that they name: `covariance`: symmetric; the masked leading block of order 512 is positive definite. `tile_mask`: symmetric; tiles on the diagonal and next to it, and tiles whose row and column both lie among the first 4 tile rows, are all ones.
All inputs are finite; a program needn't handle non-finite values.
Results may differ from the reference program's by a relative error of at most 0.001.
Values sent between devices are 32-bit elements; how exact they have to be, the bound alone decides.
No kernel may reach another device: no remote copies, remote signals or barrier semaphores. Data moves between devices by JAX's collectives and lax.ppermute only.
A program may use at most 64 MiB of HBM per device.

```python
import jax
import jax.numpy as jnp
from jax import lax

B = 128
TPP = 2
PANELS = 2
TR = 3
W = 256
LEAD = 512
NT = 24
TC = 6
NORD = 3072
N_ROW = 8
N_COL = 4


def draw_covariance(key, part):
    base = jax.random.fold_in(key, 11)
    key_sym, key_sign, key_diag = jax.random.split(base, 3)
    key_points = jax.random.fold_in(base, 37)
    entries = jax.random.uniform(key_sym, (NORD, NORD), jnp.float32, -1.0, 1.0)
    symmetric = 0.5 * (entries + entries.T)
    position = jnp.arange(NORD)
    signs = jnp.where(jax.random.uniform(key_sign, (NORD,)) < 0.5, -1.0, 1.0)
    diag_values = 1.5 + 0.5 * jax.random.uniform(key_diag, (NORD,))
    row_lead = position[:, None] < LEAD
    col_lead = position[None, :] < LEAD
    scales = jnp.ones((NORD,), jnp.float32)
    trail_part = symmetric
    far_sign = jnp.where(row_lead, signs[None, :], signs[:, None])
    far_scale = jnp.where(row_lead, scales[None, :], scales[:, None])
    panel_part = 0.08 * (0.45 * far_sign + symmetric) * far_scale
    points = jax.random.uniform(key_points, (LEAD, 3), jnp.float32, 0.0, 1.0)
    gaps = points[:, None, :] - points[None, :, :]
    distance = jnp.sqrt(gaps[:, :, 0] * gaps[:, :, 0] + gaps[:, :, 1] * gaps[:, :, 1] + gaps[:, :, 2] * gaps[:, :, 2])
    lead_block = 0.05 * jnp.exp(-distance / 0.25) + 0.025 * symmetric[:LEAD, :LEAD]
    lead_part = jnp.pad(lead_block, ((0, NORD - LEAD), (0, NORD - LEAD)))
    both_lead = jnp.logical_and(row_lead, col_lead)
    one_lead = jnp.logical_or(row_lead, col_lead)
    matrix = jnp.where(both_lead, lead_part, jnp.where(one_lead, panel_part, trail_part))
    matrix = jnp.where(position[:, None] == position[None, :], diag_values[:, None], matrix)
    tiled = jnp.transpose(matrix.reshape(NT, B, NT, B), (0, 2, 1, 3))
    return tiled.reshape(TR, N_ROW, TC, N_COL, B, B)


def draw_tile_mask(key, part):
    base = jax.random.fold_in(key, 23)
    key_level, key_roll = jax.random.split(base)
    level = jax.random.randint(key_level, (NT,), 0, 5)
    rolled = jax.random.randint(key_roll, (NT, NT), 0, 1000)
    threshold = 30 + 25 * (level[:, None] + level[None, :])
    chosen = rolled < threshold
    chosen = jnp.logical_or(chosen, chosen.T)
    tile_index = jnp.arange(NT)
    banded = jnp.abs(tile_index[:, None] - tile_index[None, :]) <= 1
    lead_tiles = PANELS * TPP
    lead_square = jnp.logical_and(tile_index[:, None] < lead_tiles, tile_index[None, :] < lead_tiles)
    return jnp.logical_or(jnp.logical_or(chosen, banded), lead_square).astype(jnp.int32)


def setup_inputs(seed: int = 0) -> dict:
    splits = jax.random.split(jax.random.key(seed), 3)
    covariance = draw_covariance(jax.random.fold_in(splits[2], 71), 0)
    tile_mask = draw_tile_mask(jax.random.fold_in(splits[2], 71), 0)
    return {"covariance": covariance, "tile_mask": tile_mask}


def assemble(covariance, tile_mask):
    tiles = covariance.reshape(NT, NT, B, B) * tile_mask.astype(jnp.float32)[:, :, None, None]
    return jnp.transpose(tiles, (0, 2, 1, 3)).reshape(NORD, NORD)

def reference(covariance, tile_mask):
    matrix = assemble(covariance, tile_mask)
    columns = []
    for panel_index in range(PANELS):
        diag_block = matrix[:W, :W]
        lower_factor = jnp.linalg.cholesky(diag_block)
        below = lax.linalg.triangular_solve(lower_factor, matrix[W:, :W], left_side=False, lower=True, transpose_a=True)
        above_zero = jnp.zeros((panel_index * W, W), jnp.float32)
        columns.append(jnp.concatenate([above_zero, lower_factor, below], axis=0))
        matrix = matrix[W:, W:] - jnp.dot(below.astype(jnp.float32), below.T.astype(jnp.float32), precision=lax.Precision.HIGHEST, preferred_element_type=jnp.float32)
    factor_part = jnp.concatenate(columns, axis=1)
    top_rows = jnp.concatenate([factor_part[:LEAD], jnp.zeros((LEAD, NORD - LEAD), jnp.float32)], axis=1)
    bottom_rows = jnp.concatenate([factor_part[LEAD:], matrix], axis=1)
    natural = jnp.concatenate([top_rows, bottom_rows], axis=0)
    tiled = jnp.transpose(natural.reshape(NT, B, NT, B), (0, 2, 1, 3))
    return tiled.reshape(TR, N_ROW, TC, N_COL, B, B).astype(jnp.bfloat16)
```

```python
import functools

import jax
import jax.numpy as jnp
from jax import lax
from jax.experimental import pallas as pl
from jax.experimental.pallas import tpu as pltpu
from jax.sharding import PartitionSpec as P

LEAD_TILES = 4
GROUP = 16
HIGHEST = lax.Precision.HIGHEST
VMEM = pl.BlockSpec(memory_space=pltpu.VMEM)
SMEM = pl.BlockSpec(memory_space=pltpu.SMEM)


def dot(a, b):
    return lax.dot_general(a, b, (((1,), (0,)), ((), ())), precision=HIGHEST, preferred_element_type=jnp.float32)


def dot_t(a, b):
    return lax.dot_general(a, b, (((1,), (1,)), ((), ())), precision=HIGHEST, preferred_element_type=jnp.float32)


def twice(a):
    return jnp.concatenate([a, a], axis=1)


def factor_tile(tile, u_ref, w_ref):
    n = tile.shape[0]
    row = lax.broadcasted_iota(jnp.int32, (n, n), 0)
    col = lax.broadcasted_iota(jnp.int32, (n, n), 1)
    w_ref[:, :n] = tile
    w_ref[:, n:] = jnp.where(row == col, 1.0, 0.0).astype(jnp.float32)
    row_1 = lax.broadcasted_iota(jnp.int32, (GROUP, n), 0)
    row_2 = lax.broadcasted_iota(jnp.int32, (GROUP, 2 * n), 0)
    group = w_ref[:GROUP, :]
    for first in range(0, n, GROUP):
        after = first + GROUP
        column = [jnp.broadcast_to(group[:, first + k : first + k + 1], (GROUP, n)) for k in range(GROUP)]
        if after < n:
            ahead = w_ref[after : after + GROUP, :]
            ahead_column = [jnp.broadcast_to(ahead[:, first + k : first + k + 1], (GROUP, n)) for k in range(GROUP)]
        for k in range(GROUP):
            pivot = jnp.broadcast_to(column[k][k : k + 1, :], (GROUP, n))
            inverse = 1.0 / pivot
            u_ref[first + k : first + k + 1, :] = group[k : k + 1, :] * twice(lax.rsqrt(pivot[:1]))
            scaled = jnp.broadcast_to(group[k : k + 1, :], (GROUP, 2 * n)) * twice(inverse)
            group = jnp.where(row_2 == k, scaled, group - twice(column[k]) * scaled)
            for m in range(k + 1, GROUP):
                scaled = jnp.broadcast_to(column[m][k : k + 1, :], (GROUP, n)) * inverse
                column[m] = jnp.where(row_1 == k, scaled, column[m] - column[k] * scaled)
        if after < n:
            reduced = group
            group = ahead
            for k in range(GROUP):
                group = group - twice(ahead_column[k]) * jnp.broadcast_to(reduced[k : k + 1, :], (GROUP, 2 * n))
            if after + GROUP < n:
                rest = w_ref[after + GROUP :, :]
                w_ref[after + GROUP :, :] = rest - dot(rest[:, first:after], reduced)


def factor_kernel(a_ref, l_ref, k_ref, w_ref, u_ref, s_ref):
    tiles, _, n, _ = a_ref.shape
    row = lax.broadcasted_iota(jnp.int32, (n, n), 0)
    col = lax.broadcasted_iota(jnp.int32, (n, n), 1)
    zero = jnp.zeros((n, n), jnp.float32)

    def at(i):
        return slice(i * n, (i + 1) * n)

    for i in range(tiles):
        for j in range(i + 1):
            s_ref[i, j] = a_ref[i, j]
    for b in range(tiles):
        factor_tile(s_ref[b, b], u_ref.at[b], w_ref)
        inverse = u_ref[b, :, n:]
        l_ref[at(b), at(b)] = jnp.where(col >= row, u_ref[b, :, :n], 0.0).T
        k_ref[at(b), at(b)] = inverse
        for i in range(b + 1, tiles):
            l_ref[at(i), at(b)] = dot_t(s_ref[i, b], inverse)
            for j in range(b + 1, i + 1):
                s_ref[i, j] = s_ref[i, j] - dot_t(l_ref[at(i), at(b)], l_ref[at(j), at(b)])
        for j in range(b):
            total = dot(l_ref[at(b), at(j)], k_ref[at(j), at(j)])
            for m in range(j + 1, b):
                total = total + dot(l_ref[at(b), at(m)], k_ref[at(m), at(j)])
            k_ref[at(b), at(j)] = -dot(inverse, total)
        for j in range(b + 1, tiles):
            l_ref[at(b), at(j)] = zero
            k_ref[at(b), at(j)] = zero


def factor(lead):
    tiles, _, n, _ = lead.shape
    whole = jax.ShapeDtypeStruct((tiles * n, tiles * n), jnp.float32)
    return pl.pallas_call(
        factor_kernel,
        out_shape=[whole, whole],
        in_specs=[VMEM],
        out_specs=[VMEM, VMEM],
        scratch_shapes=[
            pltpu.VMEM((n, 2 * n), jnp.float32),
            pltpu.VMEM((tiles, n, 2 * n), jnp.float32),
            pltpu.VMEM(lead.shape, jnp.float32),
        ],
        compiler_params=pltpu.CompilerParams(vmem_limit_bytes=32 * 2**20),
    )(lead)


def update_kernel(rows, cols, place_ref, mask_ref, a_ref, xr_ref, xc_ref, l_ref, k_ref, out_ref, zr_ref, zc_ref, x_ref, y_ref):
    tile_rows, tile_cols, n, _ = a_ref.shape
    lead = LEAD_TILES
    my_row, my_col = place_ref[0], place_ref[1]

    def at(i):
        return slice(i * n, (i + 1) * n)

    def mask(i, j):
        return mask_ref[i, j].astype(jnp.float32)

    first = 1 if cols == lead else 0
    for k in range(lead):
        for i in range(tile_rows):
            x_ref[at(i), at(k)] = xr_ref[k, i] * mask(i * rows + my_row, k)
        for j in range(first, tile_cols):
            y_ref[at(k), at(j - first)] = xc_ref[k, j] * mask(k, j * cols + my_col)
    half = lead * n // 2
    zr_ref[:, :half] = dot_t(x_ref[:, :half], k_ref[:half, :half])
    zr_ref[:, half:] = dot_t(x_ref[...], k_ref[half:, :])
    zc_ref[:half, :] = dot(k_ref[:half, :half], y_ref[:half, :])
    zc_ref[half:, :] = dot(k_ref[half:, :], y_ref[...])
    for i in range(tile_rows):
        in_lead = jnp.logical_and(i == 0, my_row < lead)
        product = dot(zr_ref[at(i), :], zc_ref[...])
        for j in range(first, tile_cols):
            rest = a_ref[i, j] * mask(i * rows + my_row, j * cols + my_col) - product[:, at(j - first)]
            out_ref[i, j] = jnp.where(in_lead, 0.0, rest).astype(jnp.bfloat16)
        for c in range(lead):

            @pl.when(my_col == c)
            def _():
                out_ref[i, 0] = zr_ref[at(i), at(c)].astype(jnp.bfloat16)
                if i == 0:
                    for r in range(lead):

                        @pl.when(my_row == r)
                        def _():
                            out_ref[0, 0] = l_ref[at(r), at(c)].astype(jnp.bfloat16)


def update(rows, cols, place, tile_mask, mine, from_cols, from_rows, lower, inverse):
    tile_rows, tile_cols, n, _ = mine.shape
    width = LEAD_TILES * n
    used = tile_cols - 1 if cols == LEAD_TILES else tile_cols
    return pl.pallas_call(
        functools.partial(update_kernel, rows, cols),
        out_shape=jax.ShapeDtypeStruct(mine.shape, jnp.bfloat16),
        in_specs=[SMEM, SMEM, VMEM, VMEM, VMEM, VMEM, VMEM],
        out_specs=VMEM,
        scratch_shapes=[
            pltpu.VMEM((tile_rows * n, width), jnp.float32),
            pltpu.VMEM((width, used * n), jnp.float32),
            pltpu.VMEM((tile_rows * n, width), jnp.float32),
            pltpu.VMEM((width, used * n), jnp.float32),
        ],
        compiler_params=pltpu.CompilerParams(vmem_limit_bytes=40 * 2**20),
    )(place, tile_mask, mine, from_cols, from_rows, lower, inverse)


def copy_down(value, axis):
    size, index = lax.axis_size(axis), lax.axis_index(axis)
    have = LEAD_TILES
    while have < size:
        pairs = [(i, i + have) for i in range(have) if i + have < size]
        value = jnp.where(index >= have, lax.ppermute(value, axis, pairs), value)
        have *= 2
    return value


def swap(value, axis, bit):
    size, index = lax.axis_size(axis), lax.axis_index(axis)
    other = lax.ppermute(value, axis, [(i, i ^ bit) for i in range(size)])
    upper = (index & bit) != 0
    return jnp.stack([jnp.where(upper, other, value), jnp.where(upper, value, other)])


def rotate(value, axis):
    size, index = lax.axis_size(axis), lax.axis_index(axis)
    group = LEAD_TILES
    parts = [value]
    for shift in range(1, group):
        pairs = [(i, i // group * group + (i + shift) % group) for i in range(size)]
        parts.append(lax.ppermute(value, axis, pairs))
    place = index % group
    return jnp.stack([lax.select_n((place - k) % group, *parts) for k in range(group)])


def on_device(covariance, tile_mask):
    tile_rows, _, tile_cols, _, n, _ = covariance.shape
    rows, cols = lax.axis_size("row"), lax.axis_size("col")
    mine = covariance.reshape(tile_rows, tile_cols, n, n)
    lead = copy_down(mine[0, 0], "row")
    lead = rotate(copy_down(lead, "col"), "col")
    lead = swap(swap(lead, "row", 2), "row", 1)
    lead = jnp.stack([lead[r & 1, r >> 1] for r in range(LEAD_TILES)])
    from_cols = rotate(copy_down(mine[:, 0], "col"), "col")
    from_rows = swap(swap(copy_down(mine[0], "row"), "row", 2), "row", 1)
    from_rows = jnp.stack([from_rows[r & 1, r >> 1] for r in range(LEAD_TILES)])
    lower, inverse = factor(lead)
    place = jnp.stack([lax.axis_index("row"), lax.axis_index("col")]).astype(jnp.int32)
    out = update(rows, cols, place, tile_mask, mine, from_cols, from_rows, lower, inverse)
    return out.reshape(tile_rows, 1, tile_cols, 1, n, n)


def solution(mesh):
    in_specs = (P(None, "row", None, "col", None, None), P())
    out_specs = P(None, "row", None, "col", None, None)
    return jax.shard_map(on_device, mesh=mesh, in_specs=in_specs, out_specs=out_specs, check_vma=False)
```

```python
import functools

import jax
import jax.numpy as jnp
from jax import lax
from jax.experimental import pallas as pl
from jax.experimental.pallas import tpu as pltpu
from jax.sharding import PartitionSpec as P

LEAD = 4
HALF = 2
SENT = 3
GROUP = 16
HIGHEST = lax.Precision.HIGHEST
VMEM = pl.BlockSpec(memory_space=pltpu.VMEM)
SMEM = pl.BlockSpec(memory_space=pltpu.SMEM)
ROW_BY_COL = (((1,), (0,)), ((), ()))
ROW_BY_ROW = (((1,), (1,)), ((), ()))


def dot(a, b, dims=ROW_BY_COL):
    return lax.dot_general(a, b, dims, precision=HIGHEST, preferred_element_type=jnp.float32)


def dot_t(a, b):
    return dot(a, b, ROW_BY_ROW)


def split(a):
    high = a.astype(jnp.bfloat16)
    return high, (a - high.astype(jnp.float32)).astype(jnp.bfloat16)


def dot_3(a, b, dims=ROW_BY_COL):
    def part(x, y):
        return lax.dot_general(x, y, dims, preferred_element_type=jnp.float32)

    return part(a[0], b[0]) + (part(a[0], b[1]) + part(a[1], b[0]))


def twice(a):
    return jnp.concatenate([a, a], axis=1)


def factor_tile(tile, u_ref, w_ref):
    n = tile.shape[0]
    row = lax.broadcasted_iota(jnp.int32, (n, n), 0)
    col = lax.broadcasted_iota(jnp.int32, (n, n), 1)
    w_ref[:, :n] = tile
    w_ref[:, n:] = jnp.where(row == col, 1.0, 0.0).astype(jnp.float32)
    group_row = lax.broadcasted_iota(jnp.int32, (GROUP, n), 0)
    group = w_ref[:GROUP, :]
    for first in range(0, n, GROUP):
        after = first + GROUP
        column = [jnp.broadcast_to(group[:, first + k : first + k + 1], (GROUP, n)) for k in range(GROUP)]
        if after < n:
            ahead = w_ref[after : after + GROUP, :]
            ahead_column = [jnp.broadcast_to(ahead[:, first + k : first + k + 1], (GROUP, n)) for k in range(GROUP)]
        pivots = inverses = jnp.ones((GROUP, n), jnp.float32)
        for k in range(GROUP):
            here = group_row == k
            pivot = jnp.broadcast_to(column[k][k : k + 1, :], (GROUP, n))
            inverse = 1.0 / pivot
            factors = jnp.where(here, 0.0, column[k] * inverse)
            pivots = jnp.where(here, pivot, pivots)
            inverses = jnp.where(here, inverse, inverses)
            u_ref[first + k : first + k + 1, :] = group[k : k + 1, :]
            for m in range(k + 1, GROUP):
                column[m] = column[m] - factors * jnp.broadcast_to(column[m][k : k + 1, :], (GROUP, n))
            group = group - twice(factors) * jnp.broadcast_to(group[k : k + 1, :], (GROUP, 2 * n))
        u_ref[first:after, :] = u_ref[first:after, :] * twice(lax.rsqrt(pivots))
        if after < n:
            reduced = group * twice(inverses)
            terms = [
                twice(ahead_column[k]) * jnp.broadcast_to(reduced[k : k + 1, :], (GROUP, 2 * n)) for k in range(GROUP)
            ]
            group = (ahead - sum(terms[2::2], terms[0])) - sum(terms[3::2], terms[1])
            if after + GROUP < n:
                rest = w_ref[after + GROUP :, :]
                w_ref[after + GROUP :, :] = rest - dot(rest[:, first:after], reduced)


def finish_tile(u):
    n = u.shape[0]
    row = lax.broadcasted_iota(jnp.int32, (n, n), 0)
    col = lax.broadcasted_iota(jnp.int32, (n, n), 1)
    return jnp.where(col >= row, u[:, :n], 0.0).T, u[:, n:]


def at(i, n):
    return slice(i * n, (i + 1) * n)


def factor_first(place_ref, a_ref, l_ref, k_ref, s_out_ref, w_ref, u_ref, s_ref):
    n = a_ref.shape[-1]
    my_row = place_ref[0]

    def raw(i, j):
        if (i - j) % LEAD < SENT:
            apart = (my_row ^ i) & (LEAD - 1)
            return a_ref[apart & 1, apart >> 1, (i - j) % LEAD]
        return raw(j, i).T

    for i in range(LEAD):
        for j in range(i + 1):
            s_ref[i, j] = raw(i, j)
    for b in range(HALF):
        factor_tile(s_ref[b, b], u_ref, w_ref)
        lower, inverse = finish_tile(u_ref[...])
        l_ref[at(b, n), at(b, n)] = lower
        k_ref[at(b, n), at(b, n)] = inverse
        for i in range(b + 1, LEAD):
            l_ref[at(i, n), at(b, n)] = dot_t(s_ref[i, b], inverse)
            for j in range(b + 1, i + 1):
                s_ref[i, j] = s_ref[i, j] - dot_t(l_ref[at(i, n), at(b, n)], l_ref[at(j, n), at(b, n)])
        for j in range(b):
            k_ref[at(b, n), at(j, n)] = -dot(inverse, dot(l_ref[at(b, n), at(j, n)], k_ref[at(j, n), at(j, n)]))
        for j in range(b + 1, HALF):
            l_ref[at(b, n), at(j, n)] = jnp.zeros((n, n), jnp.float32)
            k_ref[at(b, n), at(j, n)] = jnp.zeros((n, n), jnp.float32)
    for i in range(HALF, LEAD):
        for j in range(HALF, i + 1):
            s_out_ref[i - HALF, j - HALF] = s_ref[i, j]


def factor_second(s_in_ref, l_in_ref, k_in_ref, l_ref, k_ref, w_ref, u_ref, s_ref):
    n = s_in_ref.shape[-1]
    rest = LEAD - HALF
    start = HALF * n
    for i in range(rest):
        for j in range(i + 1):
            s_ref[i, j] = s_in_ref[i, j]
    for b in range(rest):
        factor_tile(s_ref[b, b], u_ref, w_ref)
        lower, inverse = finish_tile(u_ref[...])
        l_ref[at(b, n), at(b, n)] = lower
        k_ref[at(b, n), at(b + HALF, n)] = inverse
        for i in range(b + 1, rest):
            l_ref[at(i, n), at(b, n)] = dot_t(s_ref[i, b], inverse)
            for j in range(b + 1, i + 1):
                s_ref[i, j] = s_ref[i, j] - dot_t(l_ref[at(i, n), at(b, n)], l_ref[at(j, n), at(b, n)])
        total = dot(l_in_ref[at(b + HALF, n), :], k_in_ref[...])
        for m in range(b):
            total = total + dot(l_ref[at(b, n), at(m, n)], k_ref[at(m, n), :start])
        k_ref[at(b, n), :start] = -dot(inverse, total)
        for j in range(b):
            k_ref[at(b, n), at(j + HALF, n)] = -dot(inverse, dot(l_ref[at(b, n), at(j, n)], k_ref[at(j, n), at(j + HALF, n)]))
        for j in range(b + 1, rest):
            l_ref[at(b, n), at(j, n)] = jnp.zeros((n, n), jnp.float32)
            k_ref[at(b, n), at(j + HALF, n)] = jnp.zeros((n, n), jnp.float32)


def factor_call(kernel, in_specs, out_shapes, n):
    return pl.pallas_call(
        kernel,
        out_shape=[jax.ShapeDtypeStruct(shape, jnp.float32) for shape in out_shapes],
        in_specs=in_specs,
        out_specs=[VMEM] * len(out_shapes),
        scratch_shapes=[
            pltpu.VMEM((n, 2 * n), jnp.float32),
            pltpu.VMEM((n, 2 * n), jnp.float32),
            pltpu.VMEM((LEAD, LEAD, n, n), jnp.float32),
        ],
        compiler_params=pltpu.CompilerParams(vmem_limit_bytes=32 * 2**20),
        cost_estimate=pl.CostEstimate(flops=8 * 10**9, bytes_accessed=2**20, transcendentals=0),
    )


def update_kernel(
    rows, cols, place_ref, mask_ref, a_ref, xr_ref, xc_ref, l1_ref, k1_ref, l2_ref, k2_ref, out_ref, x_ref, y_ref, zr_ref, zc_ref
):
    tile_rows, tile_cols, n, _ = a_ref.shape
    my_row, my_col = place_ref[0], place_ref[1]
    skip = 1 if cols == LEAD else 0
    half = HALF * n

    def mask(i, j):
        return mask_ref[i, j].astype(jnp.float32)

    def pair(ref, rows_at, cols_at):
        return ref[0, rows_at, cols_at], ref[1, rows_at, cols_at]

    def put(ref, rows_at, cols_at, value):
        ref[0, rows_at, cols_at], ref[1, rows_at, cols_at] = split(value)

    for k in range(LEAD):
        for i in range(tile_rows):
            put(x_ref, at(i, n), at(k, n), xr_ref[(my_col - k) & (LEAD - 1), i] * mask(i * rows + my_row, k))
        apart = (my_row ^ k) & (LEAD - 1)
        for j in range(skip, tile_cols):
            put(y_ref, at(k, n), at(j - skip, n), xc_ref[apart & 1, apart >> 1, j - skip] * mask(k, j * cols + my_col))
    every = slice(None)
    head, tail = slice(0, half), slice(half, LEAD * n)
    k1, k2 = split(k1_ref[...]), split(k2_ref[...])
    zr1 = dot_3(pair(x_ref, every, head), k1, ROW_BY_ROW)
    zr2 = dot_3(pair(x_ref, every, every), k2, ROW_BY_ROW)
    put(zr_ref, every, head, zr1)
    put(zr_ref, every, tail, zr2)
    put(zc_ref, head, every, dot_3(k1, pair(y_ref, head, every)))
    put(zc_ref, tail, every, dot_3(k2, pair(y_ref, every, every)))
    for i in range(tile_rows):
        in_lead = jnp.logical_and(i == 0, my_row < LEAD)
        product = dot_3(pair(zr_ref, at(i, n), every), pair(zc_ref, every, every))
        for j in range(skip, tile_cols):
            rest = a_ref[i, j] * mask(i * rows + my_row, j * cols + my_col) - product[:, at(j - skip, n)]
            out_ref[i, j] = jnp.where(in_lead, 0.0, rest).astype(jnp.bfloat16)
        for c in range(LEAD):
            z = (zr1 if c < HALF else zr2)[at(i, n), at(c % HALF, n)].astype(jnp.bfloat16)

            @pl.when(my_col == c)
            def _():
                out_ref[i, 0] = z
                if i == 0:
                    for r in range(LEAD):

                        @pl.when(my_row == r)
                        def _():
                            if c < HALF:
                                out_ref[0, 0] = l1_ref[at(r, n), at(c, n)].astype(jnp.bfloat16)
                            elif r < HALF:
                                out_ref[0, 0] = jnp.zeros((n, n), jnp.bfloat16)
                            else:
                                out_ref[0, 0] = l2_ref[at(r - HALF, n), at(c - HALF, n)].astype(jnp.bfloat16)


def update(rows, cols, place, tile_mask, mine, from_cols, from_rows, factors):
    tile_rows, tile_cols, n, _ = mine.shape
    width = LEAD * n
    used = tile_cols - 1 if cols == LEAD else tile_cols
    return pl.pallas_call(
        functools.partial(update_kernel, rows, cols),
        out_shape=jax.ShapeDtypeStruct(mine.shape, jnp.bfloat16),
        in_specs=[SMEM, SMEM] + [VMEM] * 7,
        out_specs=VMEM,
        scratch_shapes=[
            pltpu.VMEM((2, tile_rows * n, width), jnp.bfloat16),
            pltpu.VMEM((2, width, used * n), jnp.bfloat16),
            pltpu.VMEM((2, tile_rows * n, width), jnp.bfloat16),
            pltpu.VMEM((2, width, used * n), jnp.bfloat16),
        ],
        compiler_params=pltpu.CompilerParams(vmem_limit_bytes=40 * 2**20),
        cost_estimate=pl.CostEstimate(flops=4 * 10**9, bytes_accessed=2**22, transcendentals=0),
    )(place, tile_mask, mine, from_cols, from_rows, *factors)


def copy_down(value, axis):
    size, index = lax.axis_size(axis), lax.axis_index(axis)
    have = LEAD
    while have < size:
        pairs = [(i, i + have) for i in range(have) if i + have < size]
        value = jnp.where(index >= have, lax.ppermute(value, axis, pairs), value)
        have *= 2
    return value


def swap(value, axis, bit):
    size = lax.axis_size(axis)
    return [value, lax.ppermute(value, axis, [(i, i ^ bit) for i in range(size)])]


def rotate(value, wanted):
    rows, cols = lax.axis_size("row"), lax.axis_size("col")
    parts = [value]
    for shift in range(1, LEAD):
        pairs = [
            (r * cols + c, r * cols + c // LEAD * LEAD + (c + shift) % LEAD)
            for r in range(rows)
            for c in range(cols)
            if wanted(r, c)
        ]
        parts.append(lax.ppermute(value, ("row", "col"), pairs))
    return parts


def on_device(covariance, tile_mask):
    tile_rows, _, tile_cols, _, n, _ = covariance.shape
    rows, cols = lax.axis_size("row"), lax.axis_size("col")
    my_row, my_col = lax.axis_index("row"), lax.axis_index("col")
    mine = covariance.reshape(tile_rows, tile_cols, n, n)
    place = jnp.stack([my_row, my_col]).astype(jnp.int32)
    skip = 1 if cols == LEAD else 0
    lead = copy_down(mine[0, 0], "row")
    lead, across = lax.optimization_barrier((lead, mine[0, skip:]))
    across = copy_down(across, "row")
    parts = rotate(copy_down(lead, "col"), lambda r, c: (r - c) % LEAD < SENT)
    start = (my_col - my_row) % LEAD
    lead = lax.dynamic_slice_in_dim(jnp.stack(parts + parts[: SENT - 1]), start, SENT, 0)
    lead, down = lax.optimization_barrier((lead, mine[:, 0]))
    lead = jnp.stack(swap(lead, "row", 2))
    down = rotate(copy_down(down, "col"), lambda r, c: True)
    lead, across = lax.optimization_barrier((lead, across))
    lead = jnp.stack(swap(lead, "row", 1))
    across = swap(across, "row", 2)
    whole, half = LEAD * n, HALF * n
    l1, k1, s = factor_call(
        factor_first, [SMEM, VMEM], [(whole, half), (half, half), (LEAD - HALF, LEAD - HALF, n, n)], n
    )(place, lead)
    s, *across = lax.optimization_barrier((s, *across))
    across = jnp.stack(swap(jnp.stack(across), "row", 1))
    l2, k2 = factor_call(factor_second, [VMEM] * 3, [(whole - half, whole - half), (whole - half, whole)], n)(s, l1, k1)
    l2, *down = lax.optimization_barrier((l2, *down))
    down = jnp.stack(down)
    out = update(rows, cols, place, tile_mask, mine, down, across, (l1, k1, l2, k2))
    return out.reshape(tile_rows, 1, tile_cols, 1, n, n)


def solution(mesh):
    in_specs = (P(None, "row", None, "col", None, None), P())
    out_specs = P(None, "row", None, "col", None, None)
    return jax.shard_map(on_device, mesh=mesh, in_specs=in_specs, out_specs=out_specs, check_vma=False)
```

```python
import functools

import jax
import jax.numpy as jnp
from jax import lax
from jax.experimental import pallas as pl
from jax.experimental.pallas import tpu as pltpu
from jax.sharding import PartitionSpec as P

LEAD = 4
HALF = 2
COST = (4, 4, 4, 8)
GROUP = 16
HIGHEST = lax.Precision.HIGHEST
VMEM = pl.BlockSpec(memory_space=pltpu.VMEM)
SMEM = pl.BlockSpec(memory_space=pltpu.SMEM)
ROW_BY_COL = (((1,), (0,)), ((), ()))
ROW_BY_ROW = (((1,), (1,)), ((), ()))


def dot(a, b, dims=ROW_BY_COL):
    return lax.dot_general(a, b, dims, precision=HIGHEST, preferred_element_type=jnp.float32)


def dot_t(a, b):
    return dot(a, b, ROW_BY_ROW)


def split(a):
    high = a.astype(jnp.bfloat16)
    return high, (a - high.astype(jnp.float32)).astype(jnp.bfloat16)


def dot_3(a, b, dims=ROW_BY_COL):
    def part(x, y):
        return lax.dot_general(x, y, dims, preferred_element_type=jnp.float32)

    return part(a[0], b[0]) + (part(a[0], b[1]) + part(a[1], b[0]))


def twice(a):
    return jnp.concatenate([a, a], axis=1)


def factor_tile(tile, u_ref, w_ref):
    n = tile.shape[0]
    row = lax.broadcasted_iota(jnp.int32, (n, n), 0)
    col = lax.broadcasted_iota(jnp.int32, (n, n), 1)
    w_ref[:, :n] = tile
    w_ref[:, n:] = jnp.where(row == col, 1.0, 0.0).astype(jnp.float32)
    group_row = lax.broadcasted_iota(jnp.int32, (GROUP, n), 0)
    group = w_ref[:GROUP, :]
    for first in range(0, n, GROUP):
        after = first + GROUP
        column = [jnp.broadcast_to(group[:, first + k : first + k + 1], (GROUP, n)) for k in range(GROUP)]
        if after < n:
            ahead = w_ref[after : after + GROUP, :]
            ahead_column = [jnp.broadcast_to(ahead[:, first + k : first + k + 1], (GROUP, n)) for k in range(GROUP)]
        pivots = inverses = jnp.ones((GROUP, n), jnp.float32)
        for k in range(GROUP):
            here = group_row == k
            pivot = jnp.broadcast_to(column[k][k : k + 1, :], (GROUP, n))
            inverse = 1.0 / pivot
            factors = jnp.where(here, 0.0, column[k] * inverse)
            pivots = jnp.where(here, pivot, pivots)
            inverses = jnp.where(here, inverse, inverses)
            u_ref[first + k : first + k + 1, :] = group[k : k + 1, :]
            for m in range(k + 1, GROUP):
                column[m] = column[m] - factors * jnp.broadcast_to(column[m][k : k + 1, :], (GROUP, n))
            group = group - twice(factors) * jnp.broadcast_to(group[k : k + 1, :], (GROUP, 2 * n))
        u_ref[first:after, :] = u_ref[first:after, :] * twice(lax.rsqrt(pivots))
        if after < n:
            reduced = group * twice(inverses)
            terms = [
                twice(ahead_column[k]) * jnp.broadcast_to(reduced[k : k + 1, :], (GROUP, 2 * n)) for k in range(GROUP)
            ]
            group = (ahead - sum(terms[2::2], terms[0])) - sum(terms[3::2], terms[1])
            if after + GROUP < n:
                rest = w_ref[after + GROUP :, :]
                w_ref[after + GROUP :, :] = rest - dot(rest[:, first:after], reduced)


def finish_tile(u):
    n = u.shape[0]
    row = lax.broadcasted_iota(jnp.int32, (n, n), 0)
    col = lax.broadcasted_iota(jnp.int32, (n, n), 1)
    return jnp.where(col >= row, u[:, :n], 0.0).T, u[:, n:]


def at(i, n):
    return slice(i * n, (i + 1) * n)


def gather_lead(place_ref, a_ref, s_ref):
    my_row, my_col = place_ref[0], place_ref[1]
    my_pair = (my_row >> 1) & 1

    def own(i, j):
        return 4 * ((i ^ my_row) & 1) + ((j ^ my_col) & (LEAD - 1))

    def far(i, j):
        return 8 + 2 * ((i ^ my_row) & 1) + ((j ^ my_col) & 1)

    for i in range(LEAD):
        for j in range(i + 1):
            if i // 2 == j // 2:
                s_ref[i, j] = a_ref[jnp.where(my_pair == i // 2, own(i, j), far(i, j))]
            else:
                tile = a_ref[jnp.where(my_pair == i // 2, own(i, j), own(j, i))]
                s_ref[i, j] = jnp.where(my_pair == i // 2, tile, tile.T)


def factor_kernel(b, *refs):
    refs = list(refs)
    left = LEAD - b
    if b == 0:
        place_ref, a_ref = refs[:2]
        del refs[:2]
        l_in, k_in = [], []
    else:
        s_in = refs.pop(0)
        l_in, k_in = refs[:b], refs[b : 2 * b]
        del refs[: 2 * b]
    if b < LEAD - 1:
        l_ref, k_ref, s_out, w_ref, u_ref, s_ref = refs
    else:
        l_ref, k_ref, w_ref, u_ref, s_ref = refs
    n = l_ref.shape[-1]
    if b == 0:
        gather_lead(place_ref, a_ref, s_ref)
    else:
        s_ref[0, 0] = s_in[0, 0]
        last = l_in[b - 1]
        for i in range(1, left):
            for j in range(i + 1):
                s_ref[i, j] = s_in[i, j] - dot_t(last[at(i + 1, n), :], last[at(j + 1, n), :])
        total = dot(last[at(1, n), :], k_in[b - 1][...])
        for j in range(b - 1):
            part = dot(l_in[j][at(b - j, n), :], k_in[j][...])
            pad = jnp.zeros((n, (b - 1 - j) * n), jnp.float32)
            total = total + jnp.concatenate([part, pad], axis=1)
    factor_tile(s_ref[0, 0], u_ref, w_ref)
    lower, inverse = finish_tile(u_ref[...])
    l_ref[at(0, n), :] = lower
    for i in range(1, left):
        l_ref[at(i, n), :] = dot_t(s_ref[i, 0], inverse)
    if b < LEAD - 1:
        for i in range(1, left):
            for j in range(1, i + 1):
                s_out[i - 1, j - 1] = s_ref[i, j]
        s_out[0, 0] = s_ref[1, 1] - dot_t(l_ref[at(1, n), :], l_ref[at(1, n), :])
    if b > 0:
        k_ref[:, : b * n] = -dot(inverse, total)
    k_ref[:, b * n :] = inverse


def factor_column(b, n, place, first, l_cols, k_rows):
    left = LEAD - b
    shapes = [(left * n, n), (n, (b + 1) * n)]
    if b < LEAD - 1:
        shapes.append((left - 1, left - 1, n, n))
    args = [place, first] if b == 0 else [first, *l_cols, *k_rows]
    return pl.pallas_call(
        functools.partial(factor_kernel, b),
        out_shape=[jax.ShapeDtypeStruct(shape, jnp.float32) for shape in shapes],
        in_specs=[SMEM, VMEM] if b == 0 else [VMEM] * len(args),
        out_specs=[VMEM] * len(shapes),
        scratch_shapes=[
            pltpu.VMEM((n, 2 * n), jnp.float32),
            pltpu.VMEM((n, 2 * n), jnp.float32),
            pltpu.VMEM((left, left, n, n), jnp.float32),
        ],
        compiler_params=pltpu.CompilerParams(vmem_limit_bytes=32 * 2**20),
        cost_estimate=pl.CostEstimate(flops=COST[b] * 10**9, bytes_accessed=2**20, transcendentals=0),
    )(*args)


def update_kernel(
    rows, cols, place_ref, mask_ref, a_ref, xr_ref, xc_ref, *refs
):
    l_cols, k_rows = refs[:LEAD], refs[LEAD : 2 * LEAD]
    out_ref, x_ref, y_ref, zr_ref, zc_ref, k_ref = refs[2 * LEAD :]
    tile_rows, tile_cols, n, _ = a_ref.shape
    my_row, my_col = place_ref[0], place_ref[1]
    skip = 1 if cols == LEAD else 0
    half = HALF * n
    every = slice(None)

    def mask(i, j):
        return mask_ref[i, j].astype(jnp.float32)

    def pair(ref, rows_at, cols_at):
        return ref[0, rows_at, cols_at], ref[1, rows_at, cols_at]

    def put(ref, rows_at, cols_at, value):
        ref[0, rows_at, cols_at], ref[1, rows_at, cols_at] = split(value)

    for k in range(LEAD):
        for i in range(tile_rows):
            put(x_ref, at(i, n), at(k, n), xr_ref[(my_col ^ k) & (LEAD - 1), i] * mask(i * rows + my_row, k))
        apart = (my_row ^ k) & (LEAD - 1)
        for j in range(skip, tile_cols):
            put(y_ref, at(k, n), at(j - skip, n), xc_ref[apart & 1, apart >> 1, j - skip] * mask(k, j * cols + my_col))
    for b in range(LEAD):
        put(k_ref, at(b, n), slice(0, (b + 1) * n), k_rows[b][...])
        if b % HALF + 1 < HALF:
            k_ref[:, at(b, n), (b + 1) * n : (b // HALF + 1) * half] = jnp.zeros((2, n, n), jnp.bfloat16)
    head, tail = slice(0, half), slice(half, LEAD * n)
    k1, k2 = pair(k_ref, head, head), pair(k_ref, tail, every)
    zr1 = dot_3(pair(x_ref, every, head), k1, ROW_BY_ROW)
    zr2 = dot_3(pair(x_ref, every, every), k2, ROW_BY_ROW)
    put(zr_ref, every, head, zr1)
    put(zr_ref, every, tail, zr2)
    put(zc_ref, head, every, dot_3(k1, pair(y_ref, head, every)))
    put(zc_ref, tail, every, dot_3(k2, pair(y_ref, every, every)))
    for i in range(tile_rows):
        in_lead = jnp.logical_and(i == 0, my_row < LEAD)
        product = dot_3(pair(zr_ref, at(i, n), every), pair(zc_ref, every, every))
        for j in range(skip, tile_cols):
            rest = a_ref[i, j] * mask(i * rows + my_row, j * cols + my_col) - product[:, at(j - skip, n)]
            out_ref[i, j] = jnp.where(in_lead, 0.0, rest).astype(jnp.bfloat16)
        for c in range(LEAD):
            z = (zr1 if c < HALF else zr2)[at(i, n), at(c % HALF, n)].astype(jnp.bfloat16)

            @pl.when(my_col == c)
            def _():
                out_ref[i, 0] = z
                if i == 0:
                    for r in range(LEAD):

                        @pl.when(my_row == r)
                        def _():
                            if r >= c:
                                out_ref[0, 0] = l_cols[c][at(r - c, n), :].astype(jnp.bfloat16)
                            else:
                                out_ref[0, 0] = jnp.zeros((n, n), jnp.bfloat16)


def update(rows, cols, place, tile_mask, mine, from_cols, from_rows, factors):
    tile_rows, tile_cols, n, _ = mine.shape
    width = LEAD * n
    used = tile_cols - 1 if cols == LEAD else tile_cols
    return pl.pallas_call(
        functools.partial(update_kernel, rows, cols),
        out_shape=jax.ShapeDtypeStruct(mine.shape, jnp.bfloat16),
        in_specs=[SMEM, SMEM] + [VMEM] * (3 + 2 * LEAD),
        out_specs=VMEM,
        scratch_shapes=[
            pltpu.VMEM((2, tile_rows * n, width), jnp.bfloat16),
            pltpu.VMEM((2, width, used * n), jnp.bfloat16),
            pltpu.VMEM((2, tile_rows * n, width), jnp.bfloat16),
            pltpu.VMEM((2, width, used * n), jnp.bfloat16),
            pltpu.VMEM((2, width, width), jnp.bfloat16),
        ],
        compiler_params=pltpu.CompilerParams(vmem_limit_bytes=40 * 2**20),
        cost_estimate=pl.CostEstimate(flops=4 * 10**9, bytes_accessed=2**22, transcendentals=0),
    )(place, tile_mask, mine, from_cols, from_rows, *factors)


def copy_down(value, axis):
    size, index = lax.axis_size(axis), lax.axis_index(axis)
    have = LEAD
    while have < size:
        if 2 * have == size:
            pairs = [(i, i ^ have) for i in range(size)]
        else:
            pairs = [(i, i + have) for i in range(have) if i + have < size]
        value = jnp.where(index >= have, lax.ppermute(value, axis, pairs), value)
        have *= 2
    return value


def swap(value, axis, bit):
    size = lax.axis_size(axis)
    return [value, lax.ppermute(value, axis, [(i, i ^ bit) for i in range(size)])]


def exchange(value, axis):
    size = lax.axis_size(axis)
    return [value] + [lax.ppermute(value, axis, [(i, i ^ s) for i in range(size)]) for s in range(1, LEAD)]


def on_device(covariance, tile_mask):
    tile_rows, _, tile_cols, _, n, _ = covariance.shape
    rows, cols = lax.axis_size("row"), lax.axis_size("col")
    my_row, my_col = lax.axis_index("row"), lax.axis_index("col")
    mine = covariance.reshape(tile_rows, tile_cols, n, n)
    place = jnp.stack([my_row, my_col]).astype(jnp.int32)
    skip = 1 if cols == LEAD else 0
    lead = copy_down(mine[0, 0], "row")
    _, across = lax.optimization_barrier((lead, mine[0, skip:]))
    across = copy_down(across, "row")
    lead = jnp.stack(exchange(copy_down(lead, "col"), "col"))
    _, down = lax.optimization_barrier((lead, mine[:, 0]))
    down = exchange(copy_down(down, "col"), "col")
    part = lax.dynamic_slice_in_dim(lead, (my_row ^ my_col) & 2, 2)
    lead = jnp.concatenate([lead, swap(lead, "row", 1)[1], swap(part, "row", 2)[1], swap(part, "row", 3)[1]])
    lead, across = lax.optimization_barrier((lead, across))
    across = swap(across, "row", 2)
    l_cols, k_rows = [], []
    state = lead
    for b in range(LEAD):
        column, row, *state = factor_column(b, n, place, state, l_cols, k_rows)
        l_cols.append(column)
        k_rows.append(row)
        if b == LEAD - 1:
            break
        (state,) = state
        if b == LEAD - 2:
            state, *across = lax.optimization_barrier((state, *across))
            across = swap(jnp.stack(across), "row", 1)
    row, *moved = lax.optimization_barrier((k_rows[-1], *across, *down))
    k_rows[-1] = row
    across, down = jnp.stack(moved[:2]), jnp.stack(moved[2:])
    out = update(rows, cols, place, tile_mask, mine, down, across, (*l_cols, *k_rows))
    return out.reshape(tile_rows, 1, tile_cols, 1, n, n)


def solution(mesh):
    in_specs = (P(None, "row", None, "col", None, None), P())
    out_specs = P(None, "row", None, "col", None, None)
    return jax.shard_map(on_device, mesh=mesh, in_specs=in_specs, out_specs=out_specs, check_vma=False)
```

```python
import functools

import jax
import jax.numpy as jnp
from jax import lax
from jax.experimental import pallas as pl
from jax.experimental.pallas import tpu as pltpu
from jax.sharding import PartitionSpec as P

LEAD = 4
HALF = 2
PARTS = ((0, 3), (3, 4))
COST = 8
GROUP = 16
HIGHEST = lax.Precision.HIGHEST
VMEM = pl.BlockSpec(memory_space=pltpu.VMEM)
SMEM = pl.BlockSpec(memory_space=pltpu.SMEM)
ROW_BY_COL = (((1,), (0,)), ((), ()))
ROW_BY_ROW = (((1,), (1,)), ((), ()))


def dot(a, b, dims=ROW_BY_COL):
    return lax.dot_general(a, b, dims, precision=HIGHEST, preferred_element_type=jnp.float32)


def dot_t(a, b):
    return dot(a, b, ROW_BY_ROW)


def split(a):
    high = a.astype(jnp.bfloat16)
    return high, (a - high.astype(jnp.float32)).astype(jnp.bfloat16)


def dot_3(a, b, dims=ROW_BY_COL):
    left = jnp.concatenate([a[0], a[0], a[1]], axis=1)
    right = jnp.concatenate([b[0], b[1], b[0]], axis=dims[0][1][0])
    return lax.dot_general(left, right, dims, preferred_element_type=jnp.float32)


def factor_tile(tile, k_ref, w_ref, beside):
    n = tile.shape[0]
    w_ref[...] = tile
    row = lax.broadcasted_iota(jnp.int32, (GROUP, n), 0)
    lane = lax.broadcasted_iota(jnp.int32, (GROUP, n), 1)
    group = w_ref[:GROUP, :]
    for first in range(0, n, GROUP):
        after = first + GROUP
        column = [jnp.broadcast_to(group[:, first + k : first + k + 1], (GROUP, n)) for k in range(GROUP)]
        inside = jnp.logical_and(lane >= first, lane < after)
        group = jnp.where(inside, jnp.where(lane - first == row, 1.0, 0.0), group)
        if after < n:
            ahead = w_ref[after : after + GROUP, :]
            ahead_column = [jnp.broadcast_to(ahead[:, first + k : first + k + 1], (GROUP, n)) for k in range(GROUP)]
            ahead = jnp.where(inside, 0.0, ahead)
        pivot = jnp.broadcast_to(column[0][:1, :], (GROUP, n))
        pivots = inverses = jnp.ones((GROUP, n), jnp.float32)
        for k in range(GROUP):
            here = row == k
            inverse = 1.0 / pivot
            factors = jnp.where(here, 0.0, column[k] * inverse)
            pivots = jnp.where(here, pivot, pivots)
            inverses = jnp.where(here, inverse, inverses)
            if k + 1 < GROUP:
                both = jnp.broadcast_to(column[k][k + 1 : k + 2, :], (GROUP, n)) * jnp.broadcast_to(
                    column[k + 1][k : k + 1, :], (GROUP, n)
                )
                pivot = jnp.broadcast_to(column[k + 1][k + 1 : k + 2, :], (GROUP, n)) - both * inverse
            k_ref[first + k : first + k + 1, :] = group[k : k + 1, :]
            for m in range(k + 1, GROUP):
                column[m] = column[m] - factors * jnp.broadcast_to(column[m][k : k + 1, :], (GROUP, n))
            group = group - factors * jnp.broadcast_to(group[k : k + 1, :], (GROUP, n))
        k_ref[first:after, :] = jnp.where(lane < after, k_ref[first:after, :] * lax.rsqrt(pivots), 0.0)
        if after < n:
            reduced = group * inverses
            terms = [ahead_column[k] * jnp.broadcast_to(reduced[k : k + 1, :], (GROUP, n)) for k in range(GROUP)]
            group = (ahead - sum(terms[2::2], terms[0])) - sum(terms[3::2], terms[1])
            if after + GROUP < n:
                rest = w_ref[after + GROUP :, :]
                rest_lane = lax.broadcasted_iota(jnp.int32, rest.shape, 1)
                kept = jnp.where(jnp.logical_and(rest_lane >= first, rest_lane < after), 0.0, rest)
                w_ref[after + GROUP :, :] = kept - dot(rest[:, first:after], reduced)
        share = -(-len(beside) * GROUP // (n - first))
        for step in beside[:share]:
            step()
        beside = beside[share:]


def at(i, n):
    return slice(i * n, (i + 1) * n)


def gather_lead(place_ref, a_ref, s_ref):
    my_row, my_col = place_ref[0], place_ref[1]
    my_pair = (my_row >> 1) & 1

    def own(i, j):
        return 4 * ((i ^ my_row) & 1) + ((j ^ my_col) & (LEAD - 1))

    for i in range(LEAD):
        mine = my_pair == i // 2
        for j in range(i + 1):
            if i == j:
                s_ref[i, j] = a_ref[jnp.where(mine, own(i, j), 8 + ((i ^ my_row) & 1))]
            elif i // 2 == j // 2:
                tile = a_ref[jnp.where(mine, own(i, j), 10)]
                direct = jnp.logical_or(mine, my_row & 1 == 0)
                s_ref[i, j] = jnp.where(direct, tile, tile.T)
            else:
                tile = a_ref[jnp.where(mine, own(i, j), own(j, i))]
                s_ref[i, j] = jnp.where(mine, tile, tile.T)


def factor_kernel(low, high, *refs):
    refs = list(refs)
    if low == 0:
        place_ref, a_ref = refs[:2]
        del refs[:2]
    else:
        s_in, l_in, k_in = refs[:3]
        del refs[:3]
    l_out, k_out = refs[:2]
    s_out = refs[2] if high < LEAD else None
    w_ref, u_ref, t_ref, s_ref = refs[-4:]
    n = u_ref.shape[-1]
    if low == 0:
        gather_lead(place_ref, a_ref, s_ref)
    else:
        for i in range(low, LEAD):
            for j in range(low, i + 1):
                s_ref[i, j] = s_in[i - low, j - low]

    def l_tile(i, j):
        return l_in[at(i, n), at(j, n)] if j < low else l_out[at(i, n), at(j - low, n)]

    def k_row(i):
        width = (i + 1) * n
        return k_in[at(i, n), :width] if i < low else k_out[at(i - low, n), :width]

    def l_step(i, b):
        l_out[at(i, n), at(b - low, n)] = dot_t(s_ref[i, b], u_ref[b])

    def s_step(i, j, b):
        s_ref[i, j] = s_ref[i, j] - dot_t(l_tile(i, b), l_tile(j, b))

    def t_step(b):
        total = dot(l_tile(b, b - 1), k_row(b - 1))
        for j in range(b - 1):
            pad = jnp.zeros((n, (b - 1 - j) * n), jnp.float32)
            total = total + jnp.concatenate([dot(l_tile(b, j), k_row(j)), pad], axis=1)
        t_ref[:, : b * n] = total

    def k_step(b):
        k_out[at(b - low, n), : b * n] = -dot(u_ref[b], t_ref[:, : b * n])

    def corner_step(b):
        square = (n, n)
        row, col = lax.broadcasted_iota(jnp.int32, square, 0), lax.broadcasted_iota(jnp.int32, square, 1)
        l_out[at(b, n), at(b - low, n)] = jnp.where(row >= col, dot_t(s_ref[b, b], u_ref[b]), 0.0)

    later = []
    for b in range(low, high):
        if b > 0:
            later.append(functools.partial(t_step, b))
        factor_tile(s_ref[b, b], u_ref.at[b], w_ref, later)
        k_out[at(b - low, n), b * n : (b + 1) * n] = u_ref[b]
        if b + 1 < LEAD:
            l_step(b + 1, b)
            s_step(b + 1, b + 1, b)
        later = []
        if b > 0:
            later.append(functools.partial(k_step, b))
        for i in range(b + 2, LEAD):
            later.append(functools.partial(l_step, i, b))
            for j in range(b + 1, i + 1):
                later.append(functools.partial(s_step, i, j, b))
        later.append(functools.partial(corner_step, b))
    for step in later:
        step()
    if s_out is not None:
        for i in range(high, LEAD):
            for j in range(high, i + 1):
                s_out[i - high, j - high] = s_ref[i, j]


def factor_columns(low, high, n, args):
    shapes = [(LEAD * n, (high - low) * n), ((high - low) * n, high * n)]
    if high < LEAD:
        shapes.append((LEAD - high, LEAD - high, n, n))
    return pl.pallas_call(
        functools.partial(factor_kernel, low, high),
        out_shape=[jax.ShapeDtypeStruct(shape, jnp.float32) for shape in shapes],
        in_specs=[SMEM, VMEM] if low == 0 else [VMEM] * len(args),
        out_specs=[VMEM] * len(shapes),
        scratch_shapes=[
            pltpu.VMEM((n, n), jnp.float32),
            pltpu.VMEM((LEAD, n, n), jnp.float32),
            pltpu.VMEM((n, LEAD * n), jnp.float32),
            pltpu.VMEM((LEAD, LEAD, n, n), jnp.float32),
        ],
        compiler_params=pltpu.CompilerParams(vmem_limit_bytes=32 * 2**20),
        cost_estimate=pl.CostEstimate(flops=COST * (high - low) * 10**9, bytes_accessed=2**20, transcendentals=0),
    )(*args)


def marks_at(tile_rows, tile_cols):
    return 2, 2 + tile_rows * tile_cols, 2 + tile_rows * (tile_cols + LEAD)


def update_kernel(cols, marks_ref, a_ref, xr_ref, xc_ref, *refs):
    l_cols, k_rows = refs[: len(PARTS)], refs[len(PARTS) : 2 * len(PARTS)]
    out_ref, x_ref, y_ref, z_ref, k_ref = refs[2 * len(PARTS) :]
    part = [p for p, (low, high) in enumerate(PARTS) for _ in range(low, high)]
    tile_rows, tile_cols, n, _ = a_ref.shape
    my_row, my_col = marks_ref[0], marks_ref[1]
    of_tiles, of_rows, of_cols = marks_at(tile_rows, tile_cols)
    skip = 1 if cols == LEAD else 0
    half = HALF * n
    every = slice(None)

    def mark(at_entry):
        return marks_ref[at_entry].astype(jnp.float32)

    def pair(ref, rows_at, cols_at):
        return ref[0, rows_at, cols_at], ref[1, rows_at, cols_at]

    def put(ref, rows_at, cols_at, value):
        ref[0, rows_at, cols_at], ref[1, rows_at, cols_at] = split(value)

    for k in range(LEAD):
        for i in range(tile_rows):
            put(x_ref, at(i, n), at(k, n), xr_ref[(my_col ^ k) & (LEAD - 1), i] * mark(of_rows + i * LEAD + k))
        apart = (my_row ^ k) & (LEAD - 1)
        for j in range(skip, tile_cols):
            tile = xc_ref[apart & 1, apart >> 1, j - skip] * mark(of_cols + k * tile_cols + j)
            put(y_ref, at(k, n), at(j - skip, n), tile)
    for b in range(LEAD):
        rows_of = k_rows[part[b]]
        put(k_ref, at(b, n), slice(0, (b + 1) * n), rows_of[at(b - PARTS[part[b]][0], n), : (b + 1) * n])
        if b % HALF + 1 < HALF:
            k_ref[:, at(b, n), (b + 1) * n : (b // HALF + 1) * half] = jnp.zeros((2, n, n), jnp.bfloat16)
    head, tail = slice(0, half), slice(half, LEAD * n)
    k1, k2 = pair(k_ref, head, head), pair(k_ref, tail, every)
    put(z_ref, every, head, dot_3(pair(x_ref, every, head), k1, ROW_BY_ROW))
    put(z_ref, every, tail, dot_3(pair(x_ref, every, every), k2, ROW_BY_ROW))
    z_rows = pair(z_ref, every, every)
    for first in range(skip, tile_cols, 2):
        some = range(first, min(first + 2, tile_cols))
        here = slice((first - skip) * n, (some[-1] + 1 - skip) * n)
        z_head = split(dot_3(k1, pair(y_ref, head, here)))
        z_tail = split(dot_3(k2, pair(y_ref, every, here)))
        product = dot_3(z_rows, [jnp.concatenate(parts, axis=0) for parts in zip(z_head, z_tail)])
        for i in range(tile_rows):
            in_lead = jnp.logical_and(i == 0, my_row < LEAD)
            for j in some:
                rest = a_ref[i, j] * mark(of_tiles + i * tile_cols + j) - product[at(i, n), at(j - first, n)]
                out_ref[i, j] = jnp.where(in_lead, 0.0, rest).astype(jnp.bfloat16)
    for i in range(tile_rows):
        for c in range(LEAD):

            @pl.when(my_col == c)
            def _():
                out_ref[i, 0] = z_ref[0, at(i, n), at(c, n)]
                if i == 0:
                    for r in range(LEAD):

                        @pl.when(my_row == r)
                        def _():
                            if r >= c:
                                tile = l_cols[part[c]][at(r, n), at(c - PARTS[part[c]][0], n)]
                                out_ref[0, 0] = tile.astype(jnp.bfloat16)
                            else:
                                out_ref[0, 0] = jnp.zeros((n, n), jnp.bfloat16)


def update(cols, marks, mine, from_cols, from_rows, factors):
    tile_rows, tile_cols, n, _ = mine.shape
    width = LEAD * n
    used = tile_cols - 1 if cols == LEAD else tile_cols
    return pl.pallas_call(
        functools.partial(update_kernel, cols),
        out_shape=jax.ShapeDtypeStruct(mine.shape, jnp.bfloat16),
        in_specs=[SMEM] + [VMEM] * (3 + 2 * len(PARTS)),
        out_specs=VMEM,
        scratch_shapes=[
            pltpu.VMEM((2, tile_rows * n, width), jnp.bfloat16),
            pltpu.VMEM((2, width, used * n), jnp.bfloat16),
            pltpu.VMEM((2, tile_rows * n, width), jnp.bfloat16),
            pltpu.VMEM((2, width, width), jnp.bfloat16),
        ],
        compiler_params=pltpu.CompilerParams(vmem_limit_bytes=40 * 2**20),
        cost_estimate=pl.CostEstimate(flops=4 * 10**9, bytes_accessed=2**22, transcendentals=0),
    )(marks, mine, from_cols, from_rows, *factors)


def copy_down(value, axis):
    size, index = lax.axis_size(axis), lax.axis_index(axis)
    have = LEAD
    while have < size:
        if 2 * have == size:
            pairs = [(i, i ^ have) for i in range(size)]
        else:
            pairs = [(i, i + have) for i in range(have) if i + have < size]
        value = jnp.where(index >= have, lax.ppermute(value, axis, pairs), value)
        have *= 2
    return value


def swap(value, axis, bit):
    size = lax.axis_size(axis)
    return [value, lax.ppermute(value, axis, [(i, i ^ bit) for i in range(size)])]


def exchange(value, axis):
    size = lax.axis_size(axis)
    return [value] + [lax.ppermute(value, axis, [(i, i ^ s) for i in range(size)]) for s in range(1, LEAD)]


def on_device(covariance, tile_mask):
    tile_rows, _, tile_cols, _, n, _ = covariance.shape
    rows, cols = lax.axis_size("row"), lax.axis_size("col")
    my_row, my_col = lax.axis_index("row"), lax.axis_index("col")
    mine = covariance.reshape(tile_rows, tile_cols, n, n)
    of_rows = lax.dynamic_index_in_dim(tile_mask.reshape(tile_rows, rows, -1), my_row, 1, keepdims=False)
    of_tiles = lax.dynamic_index_in_dim(of_rows.reshape(tile_rows, tile_cols, cols), my_col, 2, keepdims=False)
    of_cols = lax.dynamic_index_in_dim(tile_mask[:LEAD].reshape(LEAD, tile_cols, cols), my_col, 2, keepdims=False)
    place = jnp.stack([my_row, my_col]).astype(jnp.int32)
    marks = jnp.concatenate([place, of_tiles.reshape(-1), of_rows[:, :LEAD].reshape(-1), of_cols.reshape(-1)])
    skip = 1 if cols == LEAD else 0
    lead = copy_down(mine[0, 0], "row")
    _, across = lax.optimization_barrier((lead, mine[0, skip:]))
    across = copy_down(across, "row")
    lead = jnp.stack(exchange(copy_down(lead, "col"), "col"))
    corner = lax.dynamic_index_in_dim(lead, (my_row ^ my_col) & (LEAD - 1), 0)
    beside = lax.dynamic_index_in_dim(lead, (my_row ^ my_col ^ 1) & (LEAD - 1), 0)
    far = swap(jnp.concatenate([corner, beside]), "row", 3)[1]
    partner = swap(lead, "row", 1)[1]
    lead = jnp.concatenate([lead, partner, swap(corner, "row", 2)[1], far])
    _, down = lax.optimization_barrier((partner, mine[:, 0]))
    down = exchange(copy_down(down, "col"), "col")
    lead, across = lax.optimization_barrier((lead, across))
    across = swap(across, "row", 2)
    l_cols, k_rows = [], []
    args = [marks, lead]
    for p, (low, high) in enumerate(PARTS):
        column, row, *state = factor_columns(low, high, n, args)
        l_cols.append(column)
        k_rows.append(row)
        if high == LEAD:
            break
        if p == len(PARTS) - 2:
            state[0], *across = lax.optimization_barrier((state[0], *across))
            across = swap(jnp.stack(across), "row", 1)
        args = [state[0], jnp.concatenate(l_cols, axis=1), k_rows[0]]
    row, *moved = lax.optimization_barrier((k_rows[-1], *across, *down))
    k_rows[-1] = row
    across, down = jnp.stack(moved[:2]), jnp.stack(moved[2:])
    out = update(cols, marks, mine, down, across, (*l_cols, *k_rows))
    return out.reshape(tile_rows, 1, tile_cols, 1, n, n)


def solution(mesh):
    in_specs = (P(None, "row", None, "col", None, None), P())
    out_specs = P(None, "row", None, "col", None, None)
    return jax.shard_map(on_device, mesh=mesh, in_specs=in_specs, out_specs=out_specs, check_vma=False)
```

```python
import functools

import jax
import jax.numpy as jnp
from jax import lax
from jax.experimental import pallas as pl
from jax.experimental.pallas import tpu as pltpu
from jax.sharding import PartitionSpec as P

LEAD = 4
HALF = 2
PARTS = ((0, 3), (3, 4))
COST = 8
GROUP = 16
HIGHEST = lax.Precision.HIGHEST
VMEM = pl.BlockSpec(memory_space=pltpu.VMEM)
SMEM = pl.BlockSpec(memory_space=pltpu.SMEM)
ROW_BY_COL = (((1,), (0,)), ((), ()))
ROW_BY_ROW = (((1,), (1,)), ((), ()))


def dot(a, b, dims=ROW_BY_COL):
    return lax.dot_general(a, b, dims, precision=HIGHEST, preferred_element_type=jnp.float32)


def dot_t(a, b):
    return dot(a, b, ROW_BY_ROW)


def split(a):
    high = a.astype(jnp.bfloat16)
    return high, (a - high.astype(jnp.float32)).astype(jnp.bfloat16)


def dot_3(a, b, dims=ROW_BY_COL):
    left = jnp.concatenate([a[0], a[0], a[1]], axis=1)
    right = jnp.concatenate([b[0], b[1], b[0]], axis=dims[0][1][0])
    return lax.dot_general(left, right, dims, preferred_element_type=jnp.float32)


def factor_tile(tile, k_ref, w_ref, beside):
    n = tile.shape[0]
    w_ref[...] = tile
    row = lax.broadcasted_iota(jnp.int32, (GROUP, n), 0)
    lane = lax.broadcasted_iota(jnp.int32, (GROUP, n), 1)
    group = w_ref[:GROUP, :]
    for first in range(0, n, GROUP):
        after = first + GROUP
        column = [jnp.broadcast_to(group[:, first + k : first + k + 1], (GROUP, n)) for k in range(GROUP)]
        inside = jnp.logical_and(lane >= first, lane < after)
        group = jnp.where(inside, jnp.where(lane - first == row, 1.0, 0.0), group)
        if after < n:
            ahead = w_ref[after : after + GROUP, :]
            ahead_column = [jnp.broadcast_to(ahead[:, first + k : first + k + 1], (GROUP, n)) for k in range(GROUP)]
            ahead = jnp.where(inside, 0.0, ahead)
        pivot = jnp.broadcast_to(column[0][:1, :], (GROUP, n))
        pivots = inverses = jnp.ones((GROUP, n), jnp.float32)
        for k in range(GROUP):
            here = row == k
            inverse = 1.0 / pivot
            factors = jnp.where(here, 0.0, column[k]) * inverse
            pivots = jnp.where(here, pivot, pivots)
            inverses = jnp.where(here, inverse, inverses)
            if k + 1 < GROUP:
                both = jnp.broadcast_to(column[k][k + 1 : k + 2, :], (GROUP, n)) * jnp.broadcast_to(
                    column[k + 1][k : k + 1, :], (GROUP, n)
                )
                pivot = jnp.broadcast_to(column[k + 1][k + 1 : k + 2, :], (GROUP, n)) - both * inverse
            k_ref[first + k : first + k + 1, :] = group[k : k + 1, :]
            for m in range(k + 1, GROUP):
                column[m] = column[m] - factors * jnp.broadcast_to(column[m][k : k + 1, :], (GROUP, n))
            group = group - factors * jnp.broadcast_to(group[k : k + 1, :], (GROUP, n))
        k_ref[first:after, :] = jnp.where(lane < after, k_ref[first:after, :] * lax.rsqrt(pivots), 0.0)
        if after < n:
            reduced = group * inverses
            terms = [ahead_column[k] * jnp.broadcast_to(reduced[k : k + 1, :], (GROUP, n)) for k in range(GROUP)]
            group = (ahead - sum(terms[2::2], terms[0])) - sum(terms[3::2], terms[1])
            if after + GROUP < n:
                rest = w_ref[after + GROUP :, :]
                rest_lane = lax.broadcasted_iota(jnp.int32, rest.shape, 1)
                kept = jnp.where(jnp.logical_and(rest_lane >= first, rest_lane < after), 0.0, rest)
                w_ref[after + GROUP :, :] = kept - dot(rest[:, first:after], reduced)
        share = -(-len(beside) * GROUP // (n - first))
        for step in beside[:share]:
            step()
        beside = beside[share:]


def at(i, n):
    return slice(i * n, (i + 1) * n)


def gather_lead(place_ref, a_ref, s_ref):
    my_row, my_col = place_ref[0], place_ref[1]
    my_pair = (my_row >> 1) & 1

    def own(i, j):
        return 4 * ((i ^ my_row) & 1) + ((j ^ my_col) & (LEAD - 1))

    def step(i, j):
        mine = my_pair == i // 2
        if i == j:
            s_ref[i, j] = a_ref[jnp.where(mine, own(i, j), 8 + ((i ^ my_row) & 1))]
        elif i // 2 == j // 2:
            tile = a_ref[jnp.where(mine, own(i, j), 10)]
            direct = jnp.logical_or(mine, my_row & 1 == 0)
            s_ref[i, j] = jnp.where(direct, tile, tile.T)
        else:
            tile = a_ref[jnp.where(mine, own(i, j), own(j, i))]
            s_ref[i, j] = jnp.where(mine, tile, tile.T)

    return {(i, j): functools.partial(step, i, j) for i in range(LEAD) for j in range(i + 1)}


def factor_kernel(low, high, *refs):
    refs = list(refs)
    if low == 0:
        place_ref, a_ref = refs[:2]
        del refs[:2]
    else:
        s_in, l_in, k_in = refs[:3]
        del refs[:3]
    l_out, k_out = refs[:2]
    s_out = refs[2] if high < LEAD else None
    w_ref, u_ref, t_ref, s_ref = refs[-4:]
    n = u_ref.shape[-1]
    if low == 0:
        take = gather_lead(place_ref, a_ref, s_ref)
        take.pop((0, 0))()
    else:
        for i in range(low, LEAD):
            for j in range(low, i + 1):
                s_ref[i, j] = s_in[i - low, j - low]

    def l_tile(i, j):
        return l_in[at(i, n), at(j, n)] if j < low else l_out[at(i, n), at(j - low, n)]

    def k_row(i):
        width = (i + 1) * n
        return k_in[at(i, n), :width] if i < low else k_out[at(i - low, n), :width]

    def l_step(i, b):
        l_out[at(i, n), at(b - low, n)] = dot_t(s_ref[i, b], u_ref[b])

    def s_step(i, j, b):
        s_ref[i, j] = s_ref[i, j] - dot_t(l_tile(i, b), l_tile(j, b))

    def t_step(b):
        total = dot(l_tile(b, b - 1), k_row(b - 1))
        for j in range(b - 1):
            pad = jnp.zeros((n, (b - 1 - j) * n), jnp.float32)
            total = total + jnp.concatenate([dot(l_tile(b, j), k_row(j)), pad], axis=1)
        t_ref[:, : b * n] = total

    def k_step(b):
        k_out[at(b - low, n), : b * n] = -dot(u_ref[b], t_ref[:, : b * n])

    def corner_step(b):
        square = (n, n)
        row, col = lax.broadcasted_iota(jnp.int32, square, 0), lax.broadcasted_iota(jnp.int32, square, 1)
        l_out[at(b, n), at(b - low, n)] = jnp.where(row >= col, dot_t(s_ref[b, b], u_ref[b]), 0.0)

    later = list(take.values()) if low == 0 else []
    for b in range(low, high):
        if b > 0:
            later.append(functools.partial(t_step, b))
        factor_tile(s_ref[b, b], u_ref.at[b], w_ref, later)
        k_out[at(b - low, n), b * n : (b + 1) * n] = u_ref[b]
        if b + 1 < LEAD:
            l_step(b + 1, b)
            s_step(b + 1, b + 1, b)
        later = []
        if b > 0:
            later.append(functools.partial(k_step, b))
        for i in range(b + 2, LEAD):
            later.append(functools.partial(l_step, i, b))
            for j in range(b + 1, i + 1):
                later.append(functools.partial(s_step, i, j, b))
        later.append(functools.partial(corner_step, b))
    for step in later:
        step()
    if s_out is not None:
        for i in range(high, LEAD):
            for j in range(high, i + 1):
                s_out[i - high, j - high] = s_ref[i, j]


def factor_columns(low, high, n, args):
    shapes = [(LEAD * n, (high - low) * n), ((high - low) * n, high * n)]
    if high < LEAD:
        shapes.append((LEAD - high, LEAD - high, n, n))
    return pl.pallas_call(
        functools.partial(factor_kernel, low, high),
        out_shape=[jax.ShapeDtypeStruct(shape, jnp.float32) for shape in shapes],
        in_specs=[SMEM, VMEM] if low == 0 else [VMEM] * len(args),
        out_specs=[VMEM] * len(shapes),
        scratch_shapes=[
            pltpu.VMEM((n, n), jnp.float32),
            pltpu.VMEM((LEAD, n, n), jnp.float32),
            pltpu.VMEM((n, LEAD * n), jnp.float32),
            pltpu.VMEM((LEAD, LEAD, n, n), jnp.float32),
        ],
        compiler_params=pltpu.CompilerParams(vmem_limit_bytes=32 * 2**20),
        cost_estimate=pl.CostEstimate(flops=COST * (high - low) * 10**9, bytes_accessed=2**20, transcendentals=0),
    )(*args)


def marks_at(tile_rows, tile_cols):
    return 2, 2 + tile_rows * tile_cols, 2 + tile_rows * (tile_cols + LEAD)


def update_kernel(cols, marks_ref, a_ref, xr_ref, xc_ref, *refs):
    l_cols, k_rows = refs[: len(PARTS)], refs[len(PARTS) : 2 * len(PARTS)]
    out_ref, x_ref, y_ref, z_ref, k_ref = refs[2 * len(PARTS) :]
    part = [p for p, (low, high) in enumerate(PARTS) for _ in range(low, high)]
    tile_rows, tile_cols, n, _ = a_ref.shape
    my_row, my_col = marks_ref[0], marks_ref[1]
    of_tiles, of_rows, of_cols = marks_at(tile_rows, tile_cols)
    skip = 1 if cols == LEAD else 0
    half = HALF * n
    every = slice(None)

    def mark(at_entry):
        return marks_ref[at_entry].astype(jnp.float32)

    def pair(ref, rows_at, cols_at):
        return ref[0, rows_at, cols_at], ref[1, rows_at, cols_at]

    def put(ref, rows_at, cols_at, value):
        ref[0, rows_at, cols_at], ref[1, rows_at, cols_at] = split(value)

    for k in range(LEAD):
        for i in range(tile_rows):
            put(x_ref, at(i, n), at(k, n), xr_ref[(my_col ^ k) & (LEAD - 1), i] * mark(of_rows + i * LEAD + k))
        apart = (my_row ^ k) & (LEAD - 1)
        for j in range(skip, tile_cols):
            tile = xc_ref[apart & 1, apart >> 1, j - skip] * mark(of_cols + k * tile_cols + j)
            put(y_ref, at(k, n), at(j - skip, n), tile)
    for b in range(LEAD):
        rows_of = k_rows[part[b]]
        put(k_ref, at(b, n), slice(0, (b + 1) * n), rows_of[at(b - PARTS[part[b]][0], n), : (b + 1) * n])
        if b % HALF + 1 < HALF:
            k_ref[:, at(b, n), (b + 1) * n : (b // HALF + 1) * half] = jnp.zeros((2, n, n), jnp.bfloat16)
    head, tail = slice(0, half), slice(half, LEAD * n)
    k1, k2 = pair(k_ref, head, head), pair(k_ref, tail, every)
    put(z_ref, every, head, dot_3(pair(x_ref, every, head), k1, ROW_BY_ROW))
    put(z_ref, every, tail, dot_3(pair(x_ref, every, every), k2, ROW_BY_ROW))
    z_rows = pair(z_ref, every, every)
    z_head = split(dot_3(k1, pair(y_ref, head, every)))
    z_tail = split(dot_3(k2, pair(y_ref, every, every)))
    product = dot_3(z_rows, [jnp.concatenate(parts, axis=0) for parts in zip(z_head, z_tail)])
    for i in range(tile_rows):
        in_lead = jnp.logical_and(i == 0, my_row < LEAD)
        for j in range(skip, tile_cols):
            rest = a_ref[i, j] * mark(of_tiles + i * tile_cols + j) - product[at(i, n), at(j - skip, n)]
            out_ref[i, j] = jnp.where(in_lead, 0.0, rest).astype(jnp.bfloat16)
    for i in range(tile_rows):
        for c in range(LEAD):

            @pl.when(my_col == c)
            def _():
                out_ref[i, 0] = z_ref[0, at(i, n), at(c, n)]
                if i == 0:
                    for r in range(LEAD):

                        @pl.when(my_row == r)
                        def _():
                            if r >= c:
                                tile = l_cols[part[c]][at(r, n), at(c - PARTS[part[c]][0], n)]
                                out_ref[0, 0] = tile.astype(jnp.bfloat16)
                            else:
                                out_ref[0, 0] = jnp.zeros((n, n), jnp.bfloat16)


def update(cols, marks, mine, from_cols, from_rows, factors):
    tile_rows, tile_cols, n, _ = mine.shape
    width = LEAD * n
    used = tile_cols - 1 if cols == LEAD else tile_cols
    return pl.pallas_call(
        functools.partial(update_kernel, cols),
        out_shape=jax.ShapeDtypeStruct(mine.shape, jnp.bfloat16),
        in_specs=[SMEM] + [VMEM] * (3 + 2 * len(PARTS)),
        out_specs=VMEM,
        scratch_shapes=[
            pltpu.VMEM((2, tile_rows * n, width), jnp.bfloat16),
            pltpu.VMEM((2, width, used * n), jnp.bfloat16),
            pltpu.VMEM((2, tile_rows * n, width), jnp.bfloat16),
            pltpu.VMEM((2, width, width), jnp.bfloat16),
        ],
        compiler_params=pltpu.CompilerParams(vmem_limit_bytes=40 * 2**20),
        cost_estimate=pl.CostEstimate(flops=4 * 10**9, bytes_accessed=2**22, transcendentals=0),
    )(marks, mine, from_cols, from_rows, *factors)


def copy_down(value, axis):
    size, index = lax.axis_size(axis), lax.axis_index(axis)
    have = LEAD
    while have < size:
        if 2 * have == size:
            pairs = [(i, i ^ have) for i in range(size)]
        else:
            pairs = [(i, i + have) for i in range(have) if i + have < size]
        value = jnp.where(index >= have, lax.ppermute(value, axis, pairs), value)
        have *= 2
    return value


def swap(value, axis, bit):
    size = lax.axis_size(axis)
    return [value, lax.ppermute(value, axis, [(i, i ^ bit) for i in range(size)])]


def exchange(value, axis):
    size = lax.axis_size(axis)
    return [value] + [lax.ppermute(value, axis, [(i, i ^ s) for i in range(size)]) for s in range(1, LEAD)]


def on_device(covariance, tile_mask):
    tile_rows, _, tile_cols, _, n, _ = covariance.shape
    rows, cols = lax.axis_size("row"), lax.axis_size("col")
    my_row, my_col = lax.axis_index("row"), lax.axis_index("col")
    mine = covariance.reshape(tile_rows, tile_cols, n, n)
    of_rows = lax.dynamic_index_in_dim(tile_mask.reshape(tile_rows, rows, -1), my_row, 1, keepdims=False)
    of_tiles = lax.dynamic_index_in_dim(of_rows.reshape(tile_rows, tile_cols, cols), my_col, 2, keepdims=False)
    of_cols = lax.dynamic_index_in_dim(tile_mask[:LEAD].reshape(LEAD, tile_cols, cols), my_col, 2, keepdims=False)
    place = jnp.stack([my_row, my_col]).astype(jnp.int32)
    marks = jnp.concatenate([place, of_tiles.reshape(-1), of_rows[:, :LEAD].reshape(-1), of_cols.reshape(-1)])
    skip = 1 if cols == LEAD else 0
    lead = copy_down(mine[0, 0], "row")
    _, across = lax.optimization_barrier((lead, mine[0, skip:]))
    across = copy_down(across, "row")
    lead = jnp.stack(exchange(copy_down(lead, "col"), "col"))
    corner = lax.dynamic_index_in_dim(lead, (my_row ^ my_col) & (LEAD - 1), 0)
    beside = lax.dynamic_index_in_dim(lead, (my_row ^ my_col ^ 1) & (LEAD - 1), 0)
    far = swap(jnp.concatenate([corner, beside]), "row", 3)[1]
    partner = swap(lead, "row", 1)[1]
    lead = jnp.concatenate([lead, partner, swap(corner, "row", 2)[1], far])
    _, down = lax.optimization_barrier((partner, mine[:, 0]))
    down = exchange(copy_down(down, "col"), "col")
    _, across = lax.optimization_barrier((partner, across))
    across = swap(across, "row", 2)
    l_cols, k_rows = [], []
    args = [marks, lead]
    for p, (low, high) in enumerate(PARTS):
        column, row, *state = factor_columns(low, high, n, args)
        l_cols.append(column)
        k_rows.append(row)
        if high == LEAD:
            break
        if p == len(PARTS) - 2:
            state[0], *across = lax.optimization_barrier((state[0], *across))
            across = swap(jnp.stack(across), "row", 1)
        args = [state[0], jnp.concatenate(l_cols, axis=1), k_rows[0]]
    row, *moved = lax.optimization_barrier((k_rows[-1], *across, *down))
    k_rows[-1] = row
    across, down = jnp.stack(moved[:2]), jnp.stack(moved[2:])
    out = update(cols, marks, mine, down, across, (*l_cols, *k_rows))
    return out.reshape(tile_rows, 1, tile_cols, 1, n, n)


def solution(mesh):
    in_specs = (P(None, "row", None, "col", None, None), P())
    out_specs = P(None, "row", None, "col", None, None)
    return jax.shard_map(on_device, mesh=mesh, in_specs=in_specs, out_specs=out_specs, check_vma=False)
```

```python
import functools

import jax
import jax.numpy as jnp
from jax import lax
from jax.experimental import pallas as pl
from jax.experimental.pallas import tpu as pltpu
from jax.sharding import PartitionSpec as P

LEAD = 4
HALF = 2
PARTS = ((0, 3), (3, 4))
COST = 8
LANES = 128
GROUP = 16
HIGHEST = lax.Precision.HIGHEST
VMEM = pl.BlockSpec(memory_space=pltpu.VMEM)
SMEM = pl.BlockSpec(memory_space=pltpu.SMEM)
ROW_BY_COL = (((1,), (0,)), ((), ()))
ROW_BY_ROW = (((1,), (1,)), ((), ()))


def dot(a, b, dims=ROW_BY_COL):
    if a.shape[1] < LANES:
        return lax.dot_general(a, b, dims, precision=HIGHEST, preferred_element_type=jnp.float32)
    (x, rest), (y, other) = split(a), split(b)
    x_last = (a - x.astype(jnp.float32) - rest.astype(jnp.float32)).astype(jnp.bfloat16)
    y_last = (b - y.astype(jnp.float32) - other.astype(jnp.float32)).astype(jnp.bfloat16)
    left = jnp.concatenate([x, x, rest, rest, x, x_last], axis=1)
    right = jnp.concatenate([y, other, y, other, y_last, y], axis=dims[0][1][0])
    return lax.dot_general(left, right, dims, preferred_element_type=jnp.float32)


def dot_t(a, b):
    return dot(a, b, ROW_BY_ROW)


def split(a):
    high = a.astype(jnp.bfloat16)
    return high, (a - high.astype(jnp.float32)).astype(jnp.bfloat16)


def dot_3(a, b, dims=ROW_BY_COL):
    left = jnp.concatenate([a[0], a[0], a[1]], axis=1)
    right = jnp.concatenate([b[0], b[1], b[0]], axis=dims[0][1][0])
    return lax.dot_general(left, right, dims, preferred_element_type=jnp.float32)


def factor_tile(tile, k_ref, w_ref, beside):
    n = tile.shape[0]
    w_ref[...] = tile
    row = lax.broadcasted_iota(jnp.int32, (GROUP, n), 0)
    lane = lax.broadcasted_iota(jnp.int32, (GROUP, n), 1)
    group = w_ref[:GROUP, :]
    for first in range(0, n, GROUP):
        after = first + GROUP
        column = [jnp.broadcast_to(group[:, first + k : first + k + 1], (GROUP, n)) for k in range(GROUP)]
        inside = jnp.logical_and(lane >= first, lane < after)
        group = jnp.where(inside, jnp.where(lane - first == row, 1.0, 0.0), group)
        if after < n:
            ahead = w_ref[after : after + GROUP, :]
            ahead_column = [jnp.broadcast_to(ahead[:, first + k : first + k + 1], (GROUP, n)) for k in range(GROUP)]
            ahead = jnp.where(inside, 0.0, ahead)
        pivot = jnp.broadcast_to(column[0][:1, :], (GROUP, n))
        pivots = inverses = jnp.ones((GROUP, n), jnp.float32)
        for k in range(GROUP):
            here = row == k
            inverse = 1.0 / pivot
            factors = jnp.where(here, 0.0, column[k]) * inverse
            pivots = jnp.where(here, pivot, pivots)
            inverses = jnp.where(here, inverse, inverses)
            if k + 1 < GROUP:
                both = jnp.broadcast_to(column[k][k + 1 : k + 2, :], (GROUP, n)) * jnp.broadcast_to(
                    column[k + 1][k : k + 1, :], (GROUP, n)
                )
                pivot = jnp.broadcast_to(column[k + 1][k + 1 : k + 2, :], (GROUP, n)) - both * inverse
            k_ref[first + k : first + k + 1, :] = group[k : k + 1, :]
            for m in range(k + 1, GROUP):
                column[m] = column[m] - factors * jnp.broadcast_to(column[m][k : k + 1, :], (GROUP, n))
            group = group - factors * jnp.broadcast_to(group[k : k + 1, :], (GROUP, n))
        k_ref[first:after, :] = jnp.where(lane < after, k_ref[first:after, :] * lax.rsqrt(pivots), 0.0)
        if after < n:
            reduced = group * inverses
            terms = [ahead_column[k] * jnp.broadcast_to(reduced[k : k + 1, :], (GROUP, n)) for k in range(GROUP)]
            group = (ahead - sum(terms[2::2], terms[0])) - sum(terms[3::2], terms[1])
            if after + GROUP < n:
                rest = w_ref[after + GROUP :, :]
                rest_lane = lax.broadcasted_iota(jnp.int32, rest.shape, 1)
                kept = jnp.where(jnp.logical_and(rest_lane >= first, rest_lane < after), 0.0, rest)
                w_ref[after + GROUP :, :] = kept - dot(rest[:, first:after], reduced)
        share = -(-len(beside) * GROUP // (n - first))
        for step in beside[:share]:
            step()
        beside = beside[share:]


def at(i, n):
    return slice(i * n, (i + 1) * n)


def gather_lead(place_ref, a_ref, s_ref):
    my_row, my_col = place_ref[0], place_ref[1]
    my_pair = (my_row >> 1) & 1

    def own(i, j):
        return 4 * ((i ^ my_row) & 1) + ((j ^ my_col) & (LEAD - 1))

    def step(i, j):
        mine = my_pair == i // 2
        if i == j:
            s_ref[i, j] = a_ref[jnp.where(mine, own(i, j), 8 + ((i ^ my_row) & 1))]
        elif i // 2 == j // 2:
            tile = a_ref[jnp.where(mine, own(i, j), 10)]
            direct = jnp.logical_or(mine, my_row & 1 == 0)
            s_ref[i, j] = jnp.where(direct, tile, tile.T)
        else:
            tile = a_ref[jnp.where(mine, own(i, j), own(j, i))]
            s_ref[i, j] = jnp.where(mine, tile, tile.T)

    return {(i, j): functools.partial(step, i, j) for i in range(LEAD) for j in range(i + 1)}


def factor_kernel(low, high, *refs):
    refs = list(refs)
    if low == 0:
        place_ref, a_ref = refs[:2]
        del refs[:2]
    else:
        s_in, l_in, k_in = refs[:3]
        del refs[:3]
    l_out, k_out = refs[:2]
    s_out = refs[2] if high < LEAD else None
    w_ref, u_ref, t_ref, s_ref = refs[-4:]
    n = u_ref.shape[-1]
    if low == 0:
        take = gather_lead(place_ref, a_ref, s_ref)
        take.pop((0, 0))()
    else:
        for i in range(low, LEAD):
            for j in range(low, i + 1):
                s_ref[i, j] = s_in[i - low, j - low]

    def l_tile(i, j):
        return l_in[at(i, n), at(j, n)] if j < low else l_out[at(i, n), at(j - low, n)]

    def k_row(i):
        width = (i + 1) * n
        return k_in[at(i, n), :width] if i < low else k_out[at(i - low, n), :width]

    def l_step(i, b):
        l_out[at(i, n), at(b - low, n)] = dot_t(s_ref[i, b], u_ref[b])

    def s_step(i, j, b):
        s_ref[i, j] = s_ref[i, j] - dot_t(l_tile(i, b), l_tile(j, b))

    def t_step(b):
        total = dot(l_tile(b, b - 1), k_row(b - 1))
        for j in range(b - 1):
            pad = jnp.zeros((n, (b - 1 - j) * n), jnp.float32)
            total = total + jnp.concatenate([dot(l_tile(b, j), k_row(j)), pad], axis=1)
        t_ref[:, : b * n] = total

    def k_step(b):
        k_out[at(b - low, n), : b * n] = -dot(u_ref[b], t_ref[:, : b * n])

    def corner_step(b):
        square = (n, n)
        row, col = lax.broadcasted_iota(jnp.int32, square, 0), lax.broadcasted_iota(jnp.int32, square, 1)
        l_out[at(b, n), at(b - low, n)] = jnp.where(row >= col, dot_t(s_ref[b, b], u_ref[b]), 0.0)

    later = list(take.values()) if low == 0 else []
    for b in range(low, high):
        if b > 0:
            later.append(functools.partial(t_step, b))
        factor_tile(s_ref[b, b], u_ref.at[b], w_ref, later)
        k_out[at(b - low, n), b * n : (b + 1) * n] = u_ref[b]
        if b + 1 < LEAD:
            l_step(b + 1, b)
            s_step(b + 1, b + 1, b)
        later = []
        if b > 0:
            later.append(functools.partial(k_step, b))
        for i in range(b + 2, LEAD):
            later.append(functools.partial(l_step, i, b))
            for j in range(b + 1, i + 1):
                later.append(functools.partial(s_step, i, j, b))
        later.append(functools.partial(corner_step, b))
    for step in later:
        step()
    if s_out is not None:
        for i in range(high, LEAD):
            for j in range(high, i + 1):
                s_out[i - high, j - high] = s_ref[i, j]


def factor_columns(low, high, n, args):
    shapes = [(LEAD * n, (high - low) * n), ((high - low) * n, high * n)]
    if high < LEAD:
        shapes.append((LEAD - high, LEAD - high, n, n))
    return pl.pallas_call(
        functools.partial(factor_kernel, low, high),
        out_shape=[jax.ShapeDtypeStruct(shape, jnp.float32) for shape in shapes],
        in_specs=[SMEM, VMEM] if low == 0 else [VMEM] * len(args),
        out_specs=[VMEM] * len(shapes),
        scratch_shapes=[
            pltpu.VMEM((n, n), jnp.float32),
            pltpu.VMEM((LEAD, n, n), jnp.float32),
            pltpu.VMEM((n, LEAD * n), jnp.float32),
            pltpu.VMEM((LEAD, LEAD, n, n), jnp.float32),
        ],
        compiler_params=pltpu.CompilerParams(vmem_limit_bytes=32 * 2**20),
        cost_estimate=pl.CostEstimate(flops=COST * (high - low) * 10**9, bytes_accessed=2**20, transcendentals=0),
    )(*args)


def marks_at(tile_rows, tile_cols):
    return 2, 2 + tile_rows * tile_cols, 2 + tile_rows * (tile_cols + LEAD)


def update_kernel(cols, marks_ref, a_ref, xr_ref, xc_ref, *refs):
    l_cols, k_rows = refs[: len(PARTS)], refs[len(PARTS) : 2 * len(PARTS)]
    out_ref, x_ref, y_ref, z_ref, k_ref = refs[2 * len(PARTS) :]
    part = [p for p, (low, high) in enumerate(PARTS) for _ in range(low, high)]
    tile_rows, tile_cols, n, _ = a_ref.shape
    my_row, my_col = marks_ref[0], marks_ref[1]
    of_tiles, of_rows, of_cols = marks_at(tile_rows, tile_cols)
    skip = 1 if cols == LEAD else 0
    half = HALF * n
    every = slice(None)

    def mark(at_entry):
        return marks_ref[at_entry].astype(jnp.float32)

    def pair(ref, rows_at, cols_at):
        return ref[0, rows_at, cols_at], ref[1, rows_at, cols_at]

    def put(ref, rows_at, cols_at, value):
        ref[0, rows_at, cols_at], ref[1, rows_at, cols_at] = split(value)

    for k in range(LEAD):
        for i in range(tile_rows):
            put(x_ref, at(i, n), at(k, n), xr_ref[(my_col ^ k) & (LEAD - 1), i] * mark(of_rows + i * LEAD + k))
        apart = (my_row ^ k) & (LEAD - 1)
        for j in range(skip, tile_cols):
            tile = xc_ref[apart & 1, apart >> 1, j - skip] * mark(of_cols + k * tile_cols + j)
            put(y_ref, at(k, n), at(j - skip, n), tile)
    for b in range(LEAD):
        rows_of = k_rows[part[b]]
        put(k_ref, at(b, n), slice(0, (b + 1) * n), rows_of[at(b - PARTS[part[b]][0], n), : (b + 1) * n])
        if b % HALF + 1 < HALF:
            k_ref[:, at(b, n), (b + 1) * n : (b // HALF + 1) * half] = jnp.zeros((2, n, n), jnp.bfloat16)
    head, tail = slice(0, half), slice(half, LEAD * n)
    k1, k2 = pair(k_ref, head, head), pair(k_ref, tail, every)
    put(z_ref, every, head, dot_3(pair(x_ref, every, head), k1, ROW_BY_ROW))
    put(z_ref, every, tail, dot_3(pair(x_ref, every, every), k2, ROW_BY_ROW))
    z_rows = pair(z_ref, every, every)
    z_head = split(dot_3(k1, pair(y_ref, head, every)))
    z_tail = split(dot_3(k2, pair(y_ref, every, every)))
    product = dot_3(z_rows, [jnp.concatenate(parts, axis=0) for parts in zip(z_head, z_tail)])
    for i in range(tile_rows):
        in_lead = jnp.logical_and(i == 0, my_row < LEAD)
        for j in range(skip, tile_cols):
            rest = a_ref[i, j] * mark(of_tiles + i * tile_cols + j) - product[at(i, n), at(j - skip, n)]
            out_ref[i, j] = jnp.where(in_lead, 0.0, rest).astype(jnp.bfloat16)
    for i in range(tile_rows):
        for c in range(LEAD):

            @pl.when(my_col == c)
            def _():
                out_ref[i, 0] = z_ref[0, at(i, n), at(c, n)]
                if i == 0:
                    for r in range(LEAD):

                        @pl.when(my_row == r)
                        def _():
                            if r >= c:
                                tile = l_cols[part[c]][at(r, n), at(c - PARTS[part[c]][0], n)]
                                out_ref[0, 0] = tile.astype(jnp.bfloat16)
                            else:
                                out_ref[0, 0] = jnp.zeros((n, n), jnp.bfloat16)


def update(cols, marks, mine, from_cols, from_rows, factors):
    tile_rows, tile_cols, n, _ = mine.shape
    width = LEAD * n
    used = tile_cols - 1 if cols == LEAD else tile_cols
    return pl.pallas_call(
        functools.partial(update_kernel, cols),
        out_shape=jax.ShapeDtypeStruct(mine.shape, jnp.bfloat16),
        in_specs=[SMEM] + [VMEM] * (3 + 2 * len(PARTS)),
        out_specs=VMEM,
        scratch_shapes=[
            pltpu.VMEM((2, tile_rows * n, width), jnp.bfloat16),
            pltpu.VMEM((2, width, used * n), jnp.bfloat16),
            pltpu.VMEM((2, tile_rows * n, width), jnp.bfloat16),
            pltpu.VMEM((2, width, width), jnp.bfloat16),
        ],
        compiler_params=pltpu.CompilerParams(vmem_limit_bytes=40 * 2**20),
        cost_estimate=pl.CostEstimate(flops=4 * 10**9, bytes_accessed=2**22, transcendentals=0),
    )(marks, mine, from_cols, from_rows, *factors)


def copy_down(value, axis):
    size, index = lax.axis_size(axis), lax.axis_index(axis)
    have = LEAD
    while have < size:
        if 2 * have == size:
            pairs = [(i, i ^ have) for i in range(size)]
        else:
            pairs = [(i, i + have) for i in range(have) if i + have < size]
        value = jnp.where(index >= have, lax.ppermute(value, axis, pairs), value)
        have *= 2
    return value


def swap(value, axis, bit):
    size = lax.axis_size(axis)
    return [value, lax.ppermute(value, axis, [(i, i ^ bit) for i in range(size)])]


def exchange(value, axis):
    size = lax.axis_size(axis)
    return [value] + [lax.ppermute(value, axis, [(i, i ^ s) for i in range(size)]) for s in range(1, LEAD)]


def on_device(covariance, tile_mask):
    tile_rows, _, tile_cols, _, n, _ = covariance.shape
    rows, cols = lax.axis_size("row"), lax.axis_size("col")
    my_row, my_col = lax.axis_index("row"), lax.axis_index("col")
    mine = covariance.reshape(tile_rows, tile_cols, n, n)
    of_rows = lax.dynamic_index_in_dim(tile_mask.reshape(tile_rows, rows, -1), my_row, 1, keepdims=False)
    of_tiles = lax.dynamic_index_in_dim(of_rows.reshape(tile_rows, tile_cols, cols), my_col, 2, keepdims=False)
    of_cols = lax.dynamic_index_in_dim(tile_mask[:LEAD].reshape(LEAD, tile_cols, cols), my_col, 2, keepdims=False)
    place = jnp.stack([my_row, my_col]).astype(jnp.int32)
    marks = jnp.concatenate([place, of_tiles.reshape(-1), of_rows[:, :LEAD].reshape(-1), of_cols.reshape(-1)])
    skip = 1 if cols == LEAD else 0
    lead = copy_down(mine[0, 0], "row")
    _, across = lax.optimization_barrier((lead, mine[0, skip:]))
    across = copy_down(across, "row")
    lead = jnp.stack(exchange(copy_down(lead, "col"), "col"))
    corner = lax.dynamic_index_in_dim(lead, (my_row ^ my_col) & (LEAD - 1), 0)
    beside = lax.dynamic_index_in_dim(lead, (my_row ^ my_col ^ 1) & (LEAD - 1), 0)
    far = swap(jnp.concatenate([corner, beside]), "row", 3)[1]
    partner = swap(lead, "row", 1)[1]
    lead = jnp.concatenate([lead, partner, swap(corner, "row", 2)[1], far])
    _, down = lax.optimization_barrier((partner, mine[:, 0]))
    down = exchange(copy_down(down, "col"), "col")
    _, across = lax.optimization_barrier((partner, across))
    across = swap(across, "row", 2)
    l_cols, k_rows = [], []
    args = [marks, lead]
    for p, (low, high) in enumerate(PARTS):
        column, row, *state = factor_columns(low, high, n, args)
        l_cols.append(column)
        k_rows.append(row)
        if high == LEAD:
            break
        if p == len(PARTS) - 2:
            state[0], *across = lax.optimization_barrier((state[0], *across))
            across = swap(jnp.stack(across), "row", 1)
        args = [state[0], jnp.concatenate(l_cols, axis=1), k_rows[0]]
    row, *moved = lax.optimization_barrier((k_rows[-1], *across, *down))
    k_rows[-1] = row
    across, down = jnp.stack(moved[:2]), jnp.stack(moved[2:])
    out = update(cols, marks, mine, down, across, (*l_cols, *k_rows))
    return out.reshape(tile_rows, 1, tile_cols, 1, n, n)


def solution(mesh):
    in_specs = (P(None, "row", None, "col", None, None), P())
    out_specs = P(None, "row", None, "col", None, None)
    return jax.shard_map(on_device, mesh=mesh, in_specs=in_specs, out_specs=out_specs, check_vma=False)
```

```python
import functools

import jax
import jax.numpy as jnp
from jax import lax
from jax.experimental import pallas as pl
from jax.experimental.pallas import tpu as pltpu
from jax.sharding import PartitionSpec as P

LEAD = 4
HALF = 2
PARTS = ((0, 3), (3, 4))
COST = 8
LANES = 128
GROUP = 16
HIGHEST = lax.Precision.HIGHEST
VMEM = pl.BlockSpec(memory_space=pltpu.VMEM)
SMEM = pl.BlockSpec(memory_space=pltpu.SMEM)
ROW_BY_COL = (((1,), (0,)), ((), ()))
ROW_BY_ROW = (((1,), (1,)), ((), ()))


def dot(a, b, dims=ROW_BY_COL):
    if a.shape[1] < LANES:
        return lax.dot_general(a, b, dims, precision=HIGHEST, preferred_element_type=jnp.float32)
    (x, rest), (y, other) = split(a), split(b)
    x_last = (a - x.astype(jnp.float32) - rest.astype(jnp.float32)).astype(jnp.bfloat16)
    y_last = (b - y.astype(jnp.float32) - other.astype(jnp.float32)).astype(jnp.bfloat16)
    left = jnp.concatenate([x, x, rest, rest, x, x_last], axis=1)
    right = jnp.concatenate([y, other, y, other, y_last, y], axis=dims[0][1][0])
    return lax.dot_general(left, right, dims, preferred_element_type=jnp.float32)


def dot_t(a, b):
    return dot(a, b, ROW_BY_ROW)


def split(a):
    high = a.astype(jnp.bfloat16)
    return high, (a - high.astype(jnp.float32)).astype(jnp.bfloat16)


def dot_3(a, b, dims=ROW_BY_COL):
    left = jnp.concatenate([a[0], a[0], a[1]], axis=1)
    right = jnp.concatenate([b[0], b[1], b[0]], axis=dims[0][1][0])
    return lax.dot_general(left, right, dims, preferred_element_type=jnp.float32)


def factor_tile(tile, k_ref, w_ref, beside):
    n = tile.shape[0]
    w_ref[...] = tile
    row = lax.broadcasted_iota(jnp.int32, (GROUP, n), 0)
    lane = lax.broadcasted_iota(jnp.int32, (GROUP, n), 1)
    group = w_ref[:GROUP, :]
    for first in range(0, n, GROUP):
        after = first + GROUP
        column = [jnp.broadcast_to(group[:, first + k : first + k + 1], (GROUP, n)) for k in range(GROUP)]
        inside = jnp.logical_and(lane >= first, lane < after)
        group = jnp.where(inside, jnp.where(lane - first == row, 1.0, 0.0), group)
        if after < n:
            ahead = w_ref[after : after + GROUP, :]
            ahead_column = [jnp.broadcast_to(ahead[:, first + k : first + k + 1], (GROUP, n)) for k in range(GROUP)]
            ahead = jnp.where(inside, 0.0, ahead)
        pivot = jnp.broadcast_to(column[0][:1, :], (GROUP, n))
        pivots = inverses = jnp.ones((GROUP, n), jnp.float32)
        for k in range(GROUP):
            here = row == k
            inverse = 1.0 / pivot
            factors = jnp.where(here, 0.0, column[k]) * inverse
            pivots = jnp.where(here, pivot, pivots)
            inverses = jnp.where(here, inverse, inverses)
            if k + 1 < GROUP:
                both = jnp.broadcast_to(column[k][k + 1 : k + 2, :], (GROUP, n)) * jnp.broadcast_to(
                    column[k + 1][k : k + 1, :], (GROUP, n)
                )
                pivot = jnp.broadcast_to(column[k + 1][k + 1 : k + 2, :], (GROUP, n)) - both * inverse
            k_ref[first + k : first + k + 1, :] = group[k : k + 1, :]
            for m in range(k + 1, GROUP):
                column[m] = column[m] - factors * jnp.broadcast_to(column[m][k : k + 1, :], (GROUP, n))
            group = group - factors * jnp.broadcast_to(group[k : k + 1, :], (GROUP, n))
        k_ref[first:after, :] = jnp.where(lane < after, k_ref[first:after, :] * lax.rsqrt(pivots), 0.0)
        if after < n:
            reduced = group * inverses
            terms = [ahead_column[k] * jnp.broadcast_to(reduced[k : k + 1, :], (GROUP, n)) for k in range(GROUP)]
            group = (ahead - sum(terms[2::2], terms[0])) - sum(terms[3::2], terms[1])
            if after + GROUP < n:
                rest = w_ref[after + GROUP :, :]
                rest_lane = lax.broadcasted_iota(jnp.int32, rest.shape, 1)
                kept = jnp.where(jnp.logical_and(rest_lane >= first, rest_lane < after), 0.0, rest)
                w_ref[after + GROUP :, :] = kept - dot(rest[:, first:after], reduced)
        share = -(-len(beside) * GROUP // (n - first))
        for step in beside[:share]:
            step()
        beside = beside[share:]


def at(i, n):
    return slice(i * n, (i + 1) * n)


def gather_lead(place_ref, a_ref, s_ref):
    my_row, my_col = place_ref[0], place_ref[1]
    my_pair = (my_row >> 1) & 1

    def own(i, j):
        return 4 * ((i ^ my_row) & 1) + ((j ^ my_col) & (LEAD - 1))

    def step(i, j):
        mine = my_pair == i // 2
        if i == j:
            s_ref[i, j] = a_ref[jnp.where(mine, own(i, j), 8 + ((i ^ my_row) & 1))]
        elif i // 2 == j // 2:
            tile = a_ref[jnp.where(mine, own(i, j), 10)]
            direct = jnp.logical_or(mine, my_row & 1 == 0)
            s_ref[i, j] = jnp.where(direct, tile, tile.T)
        else:
            tile = a_ref[jnp.where(mine, own(i, j), own(j, i))]
            s_ref[i, j] = jnp.where(mine, tile, tile.T)

    return {(i, j): functools.partial(step, i, j) for i in range(LEAD) for j in range(i + 1)}


def factor_kernel(low, high, *refs):
    refs = list(refs)
    if low == 0:
        place_ref, a_ref = refs[:2]
        del refs[:2]
    else:
        s_in, l_in, k_in = refs[:3]
        del refs[:3]
    l_out, k_out = refs[:2]
    s_out = refs[2] if high < LEAD else None
    w_ref, u_ref, t_ref, s_ref = refs[-4:]
    n = u_ref.shape[-1]
    if low == 0:
        take = gather_lead(place_ref, a_ref, s_ref)
        take.pop((0, 0))()
    else:
        for i in range(low, LEAD):
            for j in range(low, i + 1):
                s_ref[i, j] = s_in[i - low, j - low]

    def l_tile(i, j):
        return l_in[at(i, n), at(j, n)] if j < low else l_out[at(i, n), at(j - low, n)]

    def k_row(i):
        width = (i + 1) * n
        return k_in[at(i, n), :width] if i < low else k_out[at(i - low, n), :width]

    def l_step(i, b):
        l_out[at(i, n), at(b - low, n)] = dot_t(s_ref[i, b], u_ref[b])

    def s_step(i, j, b):
        s_ref[i, j] = s_ref[i, j] - dot_t(l_tile(i, b), l_tile(j, b))

    def t_step(b):
        total = dot(l_tile(b, b - 1), k_row(b - 1))
        for j in range(b - 1):
            pad = jnp.zeros((n, (b - 1 - j) * n), jnp.float32)
            total = total + jnp.concatenate([dot(l_tile(b, j), k_row(j)), pad], axis=1)
        t_ref[:, : b * n] = total

    def k_step(b):
        k_out[at(b - low, n), : b * n] = -dot(u_ref[b], t_ref[:, : b * n])

    def corner_step(b):
        square = (n, n)
        row, col = lax.broadcasted_iota(jnp.int32, square, 0), lax.broadcasted_iota(jnp.int32, square, 1)
        l_out[at(b, n), at(b - low, n)] = jnp.where(row >= col, dot_t(s_ref[b, b], u_ref[b]), 0.0)

    later = list(take.values()) if low == 0 else []
    for b in range(low, high):
        if b > 0:
            later.append(functools.partial(t_step, b))
        factor_tile(s_ref[b, b], u_ref.at[b], w_ref, later)
        k_out[at(b - low, n), b * n : (b + 1) * n] = u_ref[b]
        if b + 1 < LEAD:
            l_step(b + 1, b)
            s_step(b + 1, b + 1, b)
        later = []
        if b > 0:
            later.append(functools.partial(k_step, b))
        for i in range(b + 2, LEAD):
            later.append(functools.partial(l_step, i, b))
            for j in range(b + 1, i + 1):
                later.append(functools.partial(s_step, i, j, b))
        later.append(functools.partial(corner_step, b))
    for step in later:
        step()
    if s_out is not None:
        for i in range(high, LEAD):
            for j in range(high, i + 1):
                s_out[i - high, j - high] = s_ref[i, j]


def factor_columns(low, high, n, args):
    shapes = [(LEAD * n, (high - low) * n), ((high - low) * n, high * n)]
    if high < LEAD:
        shapes.append((LEAD - high, LEAD - high, n, n))
    return pl.pallas_call(
        functools.partial(factor_kernel, low, high),
        out_shape=[jax.ShapeDtypeStruct(shape, jnp.float32) for shape in shapes],
        in_specs=[SMEM, VMEM] if low == 0 else [VMEM] * len(args),
        out_specs=[VMEM] * len(shapes),
        scratch_shapes=[
            pltpu.VMEM((n, n), jnp.float32),
            pltpu.VMEM((LEAD, n, n), jnp.float32),
            pltpu.VMEM((n, LEAD * n), jnp.float32),
            pltpu.VMEM((LEAD, LEAD, n, n), jnp.float32),
        ],
        compiler_params=pltpu.CompilerParams(vmem_limit_bytes=32 * 2**20),
        cost_estimate=pl.CostEstimate(flops=COST * (high - low) * 10**9, bytes_accessed=2**20, transcendentals=0),
    )(*args)


def marks_at(tile_rows, tile_cols):
    return 2, 2 + tile_rows * tile_cols, 2 + tile_rows * (tile_cols + LEAD)


def update_kernel(cols, marks_ref, a_ref, xr_ref, xc_ref, xc_far_ref, *refs):
    l_cols, k_rows = refs[: len(PARTS)], refs[len(PARTS) : 2 * len(PARTS)]
    out_ref, x_ref, y_ref, z_ref, k_ref, done_ref, sems = refs[2 * len(PARTS) :]
    part = [p for p, (low, high) in enumerate(PARTS) for _ in range(low, high)]
    tile_rows, tile_cols, n, _ = a_ref.shape
    my_row, my_col = marks_ref[0], marks_ref[1]
    of_tiles, of_rows, of_cols = marks_at(tile_rows, tile_cols)
    skip = 1 if cols == LEAD else 0
    half = HALF * n
    every = slice(None)

    def mark(at_entry):
        return marks_ref[at_entry].astype(jnp.float32)

    def pair(ref, rows_at, cols_at):
        return ref[0, rows_at, cols_at], ref[1, rows_at, cols_at]

    def put(ref, rows_at, cols_at, value):
        ref[0, rows_at, cols_at], ref[1, rows_at, cols_at] = split(value)

    for k in range(LEAD):
        for i in range(tile_rows):
            put(x_ref, at(i, n), at(k, n), xr_ref[(my_col ^ k) & (LEAD - 1), i] * mark(of_rows + i * LEAD + k))
        apart = (my_row ^ k) & (LEAD - 1)
        for j in range(skip, tile_cols):
            near, far = xc_ref[apart >> 1, j - skip], xc_far_ref[apart >> 1, j - skip]
            tile = jnp.where(apart & 1 == 0, near, far) * mark(of_cols + k * tile_cols + j)
            put(y_ref, at(k, n), at(j - skip, n), tile)
    for b in range(LEAD):
        rows_of = k_rows[part[b]]
        put(k_ref, at(b, n), slice(0, (b + 1) * n), rows_of[at(b - PARTS[part[b]][0], n), : (b + 1) * n])
        if b % HALF + 1 < HALF:
            k_ref[:, at(b, n), (b + 1) * n : (b // HALF + 1) * half] = jnp.zeros((2, n, n), jnp.bfloat16)
    head, tail = slice(0, half), slice(half, LEAD * n)
    k1, k2 = pair(k_ref, head, head), pair(k_ref, tail, every)
    put(z_ref, every, head, dot_3(pair(x_ref, every, head), k1, ROW_BY_ROW))
    put(z_ref, every, tail, dot_3(pair(x_ref, every, every), k2, ROW_BY_ROW))
    z_rows = pair(z_ref, every, every)

    def panel(i):
        for c in range(LEAD):

            @pl.when(my_col == c)
            def _():
                done_ref[i, 0] = z_ref[0, at(i, n), at(c, n)]
                if i == 0:
                    for r in range(LEAD):

                        @pl.when(my_row == r)
                        def _():
                            if r >= c:
                                tile = l_cols[part[c]][at(r, n), at(c - PARTS[part[c]][0], n)]
                                done_ref[0, 0] = tile.astype(jnp.bfloat16)
                            else:
                                done_ref[0, 0] = jnp.zeros((n, n), jnp.bfloat16)

    z_head = split(dot_3(k1, pair(y_ref, head, every)))
    z_tail = split(dot_3(k2, pair(y_ref, every, every)))
    product = dot_3(z_rows, [jnp.concatenate(parts, axis=0) for parts in zip(z_head, z_tail)])
    copies = []
    for i in range(tile_rows):
        in_lead = jnp.logical_and(i == 0, my_row < LEAD)
        for j in range(skip, tile_cols):
            rest = a_ref[i, j] * mark(of_tiles + i * tile_cols + j) - product[at(i, n), at(j - skip, n)]
            done_ref[i, j] = jnp.where(in_lead, 0.0, rest).astype(jnp.bfloat16)
        if skip:
            copies.append(pltpu.make_async_copy(done_ref.at[i, 1:], out_ref.at[i, 1:], sems.at[i]))
            copies[-1].start()
    for i in range(tile_rows):
        panel(i)
    panels = slice(0, 1) if skip else slice(0, tile_cols)
    copies.append(pltpu.make_async_copy(done_ref.at[:, panels], out_ref.at[:, panels], sems.at[tile_rows]))
    copies[-1].start()
    for copy in copies:
        copy.wait()


def update(cols, marks, mine, from_cols, from_rows, factors):
    tile_rows, tile_cols, n, _ = mine.shape
    width = LEAD * n
    used = tile_cols - 1 if cols == LEAD else tile_cols
    return pl.pallas_call(
        functools.partial(update_kernel, cols),
        out_shape=jax.ShapeDtypeStruct(mine.shape, jnp.bfloat16),
        in_specs=[SMEM] + [VMEM] * (4 + 2 * len(PARTS)),
        out_specs=pl.BlockSpec(memory_space=pl.ANY),
        scratch_shapes=[
            pltpu.VMEM((2, tile_rows * n, width), jnp.bfloat16),
            pltpu.VMEM((2, width, used * n), jnp.bfloat16),
            pltpu.VMEM((2, tile_rows * n, width), jnp.bfloat16),
            pltpu.VMEM((2, width, width), jnp.bfloat16),
            pltpu.VMEM(mine.shape, jnp.bfloat16),
            pltpu.SemaphoreType.DMA((tile_rows + 1,)),
        ],
        compiler_params=pltpu.CompilerParams(vmem_limit_bytes=40 * 2**20),
        cost_estimate=pl.CostEstimate(flops=4 * 10**9, bytes_accessed=2**22, transcendentals=0),
    )(marks, mine, from_cols, *from_rows, *factors)


def copy_down(value, axis):
    size, index = lax.axis_size(axis), lax.axis_index(axis)
    have = LEAD
    while have < size:
        if 2 * have == size:
            pairs = [(i, i ^ have) for i in range(size)]
        else:
            pairs = [(i, i + have) for i in range(have) if i + have < size]
        value = jnp.where(index >= have, lax.ppermute(value, axis, pairs), value)
        have *= 2
    return value


def swap(value, axis, bit):
    size = lax.axis_size(axis)
    return [value, lax.ppermute(value, axis, [(i, i ^ bit) for i in range(size)])]


def exchange(value, axis):
    size = lax.axis_size(axis)
    parts = [lax.ppermute(value, axis, [(i, i ^ s) for i in range(size)]) for s in range(LEAD - 1, 0, -1)]
    return [value] + parts[::-1]


def on_device(covariance, tile_mask):
    tile_rows, _, tile_cols, _, n, _ = covariance.shape
    rows, cols = lax.axis_size("row"), lax.axis_size("col")
    my_row, my_col = lax.axis_index("row"), lax.axis_index("col")
    mine = covariance.reshape(tile_rows, tile_cols, n, n)
    of_rows = lax.dynamic_index_in_dim(tile_mask.reshape(tile_rows, rows, -1), my_row, 1, keepdims=False)
    of_tiles = lax.dynamic_index_in_dim(of_rows.reshape(tile_rows, tile_cols, cols), my_col, 2, keepdims=False)
    of_cols = lax.dynamic_index_in_dim(tile_mask[:LEAD].reshape(LEAD, tile_cols, cols), my_col, 2, keepdims=False)
    place = jnp.stack([my_row, my_col]).astype(jnp.int32)
    marks = jnp.concatenate([place, of_tiles.reshape(-1), of_rows[:, :LEAD].reshape(-1), of_cols.reshape(-1)])
    skip = 1 if cols == LEAD else 0
    lead = copy_down(mine[0, 0], "row")
    _, across = lax.optimization_barrier((lead, mine[0, skip:]))
    across = copy_down(across, "row")
    lead = jnp.stack(exchange(copy_down(lead, "col"), "col"))
    corner = lax.dynamic_index_in_dim(lead, (my_row ^ my_col) & (LEAD - 1), 0)
    beside = lax.dynamic_index_in_dim(lead, (my_row ^ my_col ^ 1) & (LEAD - 1), 0)
    far = swap(jnp.concatenate([corner, beside]), "row", 3)[1]
    partner = swap(lead, "row", 1)[1]
    lead = jnp.concatenate([lead, partner, swap(corner, "row", 2)[1], far])
    _, down = lax.optimization_barrier((partner, mine[:, 0]))
    down = exchange(copy_down(down, "col"), "col")
    _, across = lax.optimization_barrier((partner, across))
    across = swap(across, "row", 2)
    l_cols, k_rows = [], []
    args = [marks, lead]
    for p, (low, high) in enumerate(PARTS):
        column, row, *state = factor_columns(low, high, n, args)
        l_cols.append(column)
        k_rows.append(row)
        if high == LEAD:
            break
        if p == len(PARTS) - 2:
            state[0], *across = lax.optimization_barrier((state[0], *across))
            across = swap(jnp.stack(across), "row", 1)
        args = [state[0], jnp.concatenate(l_cols, axis=1), k_rows[0]]
    row, *moved = lax.optimization_barrier((k_rows[-1], *across, *down))
    k_rows[-1] = row
    across, down = moved[:2], jnp.stack(moved[2:])
    out = update(cols, marks, mine, down, across, (*l_cols, *k_rows))
    return out.reshape(tile_rows, 1, tile_cols, 1, n, n)


def solution(mesh):
    in_specs = (P(None, "row", None, "col", None, None), P())
    out_specs = P(None, "row", None, "col", None, None)
    return jax.shard_map(on_device, mesh=mesh, in_specs=in_specs, out_specs=out_specs, check_vma=False)
```

```python
import functools

import jax
import jax.numpy as jnp
from jax import lax
from jax.experimental import pallas as pl
from jax.experimental.pallas import tpu as pltpu
from jax.sharding import PartitionSpec as P

LEAD = 4
HALF = 2
PARTS = ((0, 3), (3, 4))
COST = 8
LANES = 128
GROUP = 16
HIGHEST = lax.Precision.HIGHEST
VMEM = pl.BlockSpec(memory_space=pltpu.VMEM)
SMEM = pl.BlockSpec(memory_space=pltpu.SMEM)
ROW_BY_COL = (((1,), (0,)), ((), ()))
ROW_BY_ROW = (((1,), (1,)), ((), ()))


def dot(a, b, dims=ROW_BY_COL):
    if a.shape[1] < LANES:
        return lax.dot_general(a, b, dims, precision=HIGHEST, preferred_element_type=jnp.float32)
    (x, rest), (y, other) = split(a), split(b)
    x_last = (a - x.astype(jnp.float32) - rest.astype(jnp.float32)).astype(jnp.bfloat16)
    y_last = (b - y.astype(jnp.float32) - other.astype(jnp.float32)).astype(jnp.bfloat16)
    left = jnp.concatenate([x, x, rest, rest, x, x_last], axis=1)
    right = jnp.concatenate([y, other, y, other, y_last, y], axis=dims[0][1][0])
    return lax.dot_general(left, right, dims, preferred_element_type=jnp.float32)


def dot_t(a, b):
    return dot(a, b, ROW_BY_ROW)


def split(a):
    high = a.astype(jnp.bfloat16)
    return high, (a - high.astype(jnp.float32)).astype(jnp.bfloat16)


def dot_3(a, b, dims=ROW_BY_COL):
    left = jnp.concatenate([a[0], a[0], a[1]], axis=1)
    right = jnp.concatenate([b[0], b[1], b[0]], axis=dims[0][1][0])
    return lax.dot_general(left, right, dims, preferred_element_type=jnp.float32)


def factor_tile(tile, k_ref, w_ref, beside):
    n = tile.shape[0]
    w_ref[...] = tile
    row = lax.broadcasted_iota(jnp.int32, (GROUP, n), 0)
    lane = lax.broadcasted_iota(jnp.int32, (GROUP, n), 1)
    group = w_ref[:GROUP, :]
    for first in range(0, n, GROUP):
        after = first + GROUP
        column = [jnp.broadcast_to(group[:, first + k : first + k + 1], (GROUP, n)) for k in range(GROUP)]
        inside = jnp.logical_and(lane >= first, lane < after)
        group = jnp.where(inside, jnp.where(lane - first == row, 1.0, 0.0), group)
        if after < n:
            ahead = w_ref[after : after + GROUP, :]
            ahead_column = [jnp.broadcast_to(ahead[:, first + k : first + k + 1], (GROUP, n)) for k in range(GROUP)]
            ahead = jnp.where(inside, 0.0, ahead)
        pivot = jnp.broadcast_to(column[0][:1, :], (GROUP, n))
        pivots = inverses = jnp.ones((GROUP, n), jnp.float32)
        for k in range(GROUP):
            here = row == k
            inverse = 1.0 / pivot
            factors = jnp.where(here, 0.0, column[k]) * inverse
            pivots = jnp.where(here, pivot, pivots)
            inverses = jnp.where(here, inverse, inverses)
            if k + 1 < GROUP:
                both = jnp.broadcast_to(column[k][k + 1 : k + 2, :], (GROUP, n)) * jnp.broadcast_to(
                    column[k + 1][k : k + 1, :], (GROUP, n)
                )
                pivot = jnp.broadcast_to(column[k + 1][k + 1 : k + 2, :], (GROUP, n)) - both * inverse
            k_ref[first + k : first + k + 1, :] = group[k : k + 1, :]
            for m in range(k + 1, GROUP):
                column[m] = column[m] - factors * jnp.broadcast_to(column[m][k : k + 1, :], (GROUP, n))
            group = group - factors * jnp.broadcast_to(group[k : k + 1, :], (GROUP, n))
        k_ref[first:after, :] = jnp.where(lane < after, k_ref[first:after, :] * lax.rsqrt(pivots), 0.0)
        if after < n:
            reduced = group * inverses
            terms = [ahead_column[k] * jnp.broadcast_to(reduced[k : k + 1, :], (GROUP, n)) for k in range(GROUP)]
            group = (ahead - sum(terms[2::2], terms[0])) - sum(terms[3::2], terms[1])
            if after + GROUP < n:
                rest = w_ref[after + GROUP :, :]
                rest_lane = lax.broadcasted_iota(jnp.int32, rest.shape, 1)
                kept = jnp.where(jnp.logical_and(rest_lane >= first, rest_lane < after), 0.0, rest)
                w_ref[after + GROUP :, :] = kept - dot(rest[:, first:after], reduced)
        share = -(-len(beside) * GROUP // (n - first))
        for step in beside[:share]:
            step()
        beside = beside[share:]


def at(i, n):
    return slice(i * n, (i + 1) * n)


def gather_lead(place_ref, a_ref, s_ref):
    my_row, my_col = place_ref[0], place_ref[1]
    my_pair = (my_row >> 1) & 1

    def own(i, j):
        return 4 * ((i ^ my_row) & 1) + ((j ^ my_col) & (LEAD - 1))

    def step(i, j):
        mine = my_pair == i // 2
        if i == j:
            s_ref[i, j] = a_ref[jnp.where(mine, own(i, j), 8 + ((i ^ my_row) & 1))]
        elif i // 2 == j // 2:
            tile = a_ref[jnp.where(mine, own(i, j), 10)]
            direct = jnp.logical_or(mine, my_row & 1 == 0)
            s_ref[i, j] = jnp.where(direct, tile, tile.T)
        else:
            tile = a_ref[jnp.where(mine, own(i, j), own(j, i))]
            s_ref[i, j] = jnp.where(mine, tile, tile.T)

    return {(i, j): functools.partial(step, i, j) for i in range(LEAD) for j in range(i + 1)}


def factor_kernel(low, high, *refs):
    refs = list(refs)
    if low == 0:
        place_ref, a_ref = refs[:2]
        del refs[:2]
    else:
        s_in, l_in, k_in = refs[:3]
        del refs[:3]
    l_out, k_out = refs[:2]
    s_out = refs[2] if high < LEAD else None
    w_ref, u_ref, t_ref, s_ref = refs[-4:]
    n = u_ref.shape[-1]
    if low == 0:
        take = gather_lead(place_ref, a_ref, s_ref)
        take.pop((0, 0))()
    else:
        for i in range(low, LEAD):
            for j in range(low, i + 1):
                s_ref[i, j] = s_in[i - low, j - low]

    def l_tile(i, j):
        return l_in[at(i, n), at(j, n)] if j < low else l_out[at(i, n), at(j - low, n)]

    def k_row(i):
        width = (i + 1) * n
        return k_in[at(i, n), :width] if i < low else k_out[at(i - low, n), :width]

    def l_step(i, b):
        l_out[at(i, n), at(b - low, n)] = dot_t(s_ref[i, b], u_ref[b])

    def s_step(i, j, b):
        s_ref[i, j] = s_ref[i, j] - dot_t(l_tile(i, b), l_tile(j, b))

    def t_step(b):
        total = dot(l_tile(b, b - 1), k_row(b - 1))
        for j in range(b - 1):
            pad = jnp.zeros((n, (b - 1 - j) * n), jnp.float32)
            total = total + jnp.concatenate([dot(l_tile(b, j), k_row(j)), pad], axis=1)
        t_ref[:, : b * n] = total

    def k_step(b):
        k_out[at(b - low, n), : b * n] = -dot(u_ref[b], t_ref[:, : b * n])

    def corner_step(b):
        square = (n, n)
        row, col = lax.broadcasted_iota(jnp.int32, square, 0), lax.broadcasted_iota(jnp.int32, square, 1)
        l_out[at(b, n), at(b - low, n)] = jnp.where(row >= col, dot_t(s_ref[b, b], u_ref[b]), 0.0)

    later = list(take.values()) if low == 0 else []
    for b in range(low, high):
        if b > 0:
            later.append(functools.partial(t_step, b))
        factor_tile(s_ref[b, b], u_ref.at[b], w_ref, later)
        k_out[at(b - low, n), b * n : (b + 1) * n] = u_ref[b]
        if b + 1 < LEAD:
            l_step(b + 1, b)
            s_step(b + 1, b + 1, b)
        later = []
        if b > 0:
            later.append(functools.partial(k_step, b))
        for i in range(b + 2, LEAD):
            later.append(functools.partial(l_step, i, b))
            for j in range(b + 1, i + 1):
                later.append(functools.partial(s_step, i, j, b))
        later.append(functools.partial(corner_step, b))
    for step in later:
        step()
    if s_out is not None:
        for i in range(high, LEAD):
            for j in range(high, i + 1):
                s_out[i - high, j - high] = s_ref[i, j]


def factor_columns(low, high, n, args):
    shapes = [(LEAD * n, (high - low) * n), ((high - low) * n, high * n)]
    if high < LEAD:
        shapes.append((LEAD - high, LEAD - high, n, n))
    return pl.pallas_call(
        functools.partial(factor_kernel, low, high),
        out_shape=[jax.ShapeDtypeStruct(shape, jnp.float32) for shape in shapes],
        in_specs=[SMEM, VMEM] if low == 0 else [VMEM] * len(args),
        out_specs=[VMEM] * len(shapes),
        scratch_shapes=[
            pltpu.VMEM((n, n), jnp.float32),
            pltpu.VMEM((LEAD, n, n), jnp.float32),
            pltpu.VMEM((n, LEAD * n), jnp.float32),
            pltpu.VMEM((LEAD, LEAD, n, n), jnp.float32),
        ],
        compiler_params=pltpu.CompilerParams(vmem_limit_bytes=32 * 2**20),
        cost_estimate=pl.CostEstimate(flops=COST * (high - low) * 10**9, bytes_accessed=2**20, transcendentals=0),
    )(*args)


def marks_at(tile_rows, tile_cols):
    return 2, 2 + tile_rows * tile_cols, 2 + tile_rows * (tile_cols + LEAD)


def update_kernel(cols, marks_ref, a_ref, xr_ref, xc_ref, xc_far_ref, *refs):
    l_cols, k_rows = refs[: len(PARTS)], refs[len(PARTS) : 2 * len(PARTS)]
    out_ref, x_ref, y_ref, z_ref, k_ref, done_ref, sems = refs[2 * len(PARTS) :]
    part = [p for p, (low, high) in enumerate(PARTS) for _ in range(low, high)]
    tile_rows, tile_cols, n, _ = a_ref.shape
    my_row, my_col = marks_ref[0], marks_ref[1]
    of_tiles, of_rows, of_cols = marks_at(tile_rows, tile_cols)
    skip = 1 if cols == LEAD else 0
    half = HALF * n
    every = slice(None)

    def mark(at_entry):
        return marks_ref[at_entry].astype(jnp.float32)

    def pair(ref, rows_at, cols_at):
        return ref[0, rows_at, cols_at], ref[1, rows_at, cols_at]

    def put(ref, rows_at, cols_at, value):
        ref[0, rows_at, cols_at], ref[1, rows_at, cols_at] = split(value)

    for k in range(LEAD):
        for i in range(tile_rows):
            put(x_ref, at(i, n), at(k, n), xr_ref[(my_col ^ k) & (LEAD - 1), i] * mark(of_rows + i * LEAD + k))
        apart = (my_row ^ k) & (LEAD - 1)
        for j in range(skip, tile_cols):
            near, far = xc_ref[apart >> 1, j - skip], xc_far_ref[apart >> 1, j - skip]
            tile = jnp.where(apart & 1 == 0, near, far) * mark(of_cols + k * tile_cols + j)
            put(y_ref, at(k, n), at(j - skip, n), tile)
    for b in range(LEAD):
        rows_of = k_rows[part[b]]
        put(k_ref, at(b, n), slice(0, (b + 1) * n), rows_of[at(b - PARTS[part[b]][0], n), : (b + 1) * n])
        if b % HALF + 1 < HALF:
            k_ref[:, at(b, n), (b + 1) * n : (b // HALF + 1) * half] = jnp.zeros((2, n, n), jnp.bfloat16)
    head, tail = slice(0, half), slice(half, LEAD * n)
    k1, k2 = pair(k_ref, head, head), pair(k_ref, tail, every)
    put(z_ref, every, head, dot_3(pair(x_ref, every, head), k1, ROW_BY_ROW))
    put(z_ref, every, tail, dot_3(pair(x_ref, every, every), k2, ROW_BY_ROW))
    z_rows = pair(z_ref, every, every)

    def panel(i):
        for c in range(LEAD):

            @pl.when(my_col == c)
            def _():
                done_ref[i, 0] = z_ref[0, at(i, n), at(c, n)]
                if i == 0:
                    for r in range(LEAD):

                        @pl.when(my_row == r)
                        def _():
                            if r >= c:
                                tile = l_cols[part[c]][at(r, n), at(c - PARTS[part[c]][0], n)]
                                done_ref[0, 0] = tile.astype(jnp.bfloat16)
                            else:
                                done_ref[0, 0] = jnp.zeros((n, n), jnp.bfloat16)

    z_head = split(dot_3(k1, pair(y_ref, head, every)))
    z_tail = split(dot_3(k2, pair(y_ref, every, every)))
    product = dot_3(z_rows, [jnp.concatenate(parts, axis=0) for parts in zip(z_head, z_tail)])
    copies = []
    for i in range(tile_rows):
        in_lead = jnp.logical_and(i == 0, my_row < LEAD)
        for j in range(skip, tile_cols):
            rest = a_ref[i, j] * mark(of_tiles + i * tile_cols + j) - product[at(i, n), at(j - skip, n)]
            done_ref[i, j] = jnp.where(in_lead, 0.0, rest).astype(jnp.bfloat16)
        if skip:
            copies.append(pltpu.make_async_copy(done_ref.at[i, 1:], out_ref.at[i, 1:], sems.at[i]))
            copies[-1].start()
    for i in range(tile_rows):
        panel(i)
    panels = slice(0, 1) if skip else slice(0, tile_cols)
    copies.append(pltpu.make_async_copy(done_ref.at[:, panels], out_ref.at[:, panels], sems.at[tile_rows]))
    copies[-1].start()
    for copy in copies:
        copy.wait()


def update(cols, marks, mine, from_cols, from_rows, factors):
    tile_rows, tile_cols, n, _ = mine.shape
    width = LEAD * n
    used = tile_cols - 1 if cols == LEAD else tile_cols
    return pl.pallas_call(
        functools.partial(update_kernel, cols),
        out_shape=jax.ShapeDtypeStruct(mine.shape, jnp.bfloat16),
        in_specs=[SMEM] + [VMEM] * (4 + 2 * len(PARTS)),
        out_specs=pl.BlockSpec(memory_space=pl.ANY),
        scratch_shapes=[
            pltpu.VMEM((2, tile_rows * n, width), jnp.bfloat16),
            pltpu.VMEM((2, width, used * n), jnp.bfloat16),
            pltpu.VMEM((2, tile_rows * n, width), jnp.bfloat16),
            pltpu.VMEM((2, width, width), jnp.bfloat16),
            pltpu.VMEM(mine.shape, jnp.bfloat16),
            pltpu.SemaphoreType.DMA((tile_rows + 1,)),
        ],
        compiler_params=pltpu.CompilerParams(vmem_limit_bytes=40 * 2**20),
        cost_estimate=pl.CostEstimate(flops=4 * 10**9, bytes_accessed=2**22, transcendentals=0),
    )(marks, mine, from_cols, *from_rows, *factors)


def copy_down(value, axis):
    size, index = lax.axis_size(axis), lax.axis_index(axis)
    have = LEAD
    while have < size:
        if 2 * have == size:
            pairs = [(i, i ^ have) for i in range(size)]
        else:
            pairs = [(i, i + have) for i in range(have) if i + have < size]
        value = jnp.where(index >= have, lax.ppermute(value, axis, pairs), value)
        have *= 2
    return value


def swap(value, axis, bit):
    size = lax.axis_size(axis)
    return [value, lax.ppermute(value, axis, [(i, i ^ bit) for i in range(size)])]


def exchange(value, axis):
    size = lax.axis_size(axis)
    parts = [lax.ppermute(value, axis, [(i, i ^ s) for i in range(size)]) for s in range(LEAD - 1, 0, -1)]
    return [value] + parts[::-1]


def on_device(covariance, tile_mask):
    tile_rows, _, tile_cols, _, n, _ = covariance.shape
    rows, cols = lax.axis_size("row"), lax.axis_size("col")
    my_row, my_col = lax.axis_index("row"), lax.axis_index("col")
    mine = covariance.reshape(tile_rows, tile_cols, n, n)
    of_rows = lax.dynamic_index_in_dim(tile_mask.reshape(tile_rows, rows, -1), my_row, 1, keepdims=False)
    of_tiles = lax.dynamic_index_in_dim(of_rows.reshape(tile_rows, tile_cols, cols), my_col, 2, keepdims=False)
    of_cols = lax.dynamic_index_in_dim(tile_mask[:LEAD].reshape(LEAD, tile_cols, cols), my_col, 2, keepdims=False)
    place = jnp.stack([my_row, my_col]).astype(jnp.int32)
    marks = jnp.concatenate([place, of_tiles.reshape(-1), of_rows[:, :LEAD].reshape(-1), of_cols.reshape(-1)])
    skip = 1 if cols == LEAD else 0
    lead = copy_down(mine[0, 0], "row")
    across = copy_down(mine[0, skip:], "row")
    lead = jnp.stack(exchange(copy_down(lead, "col"), "col"))
    corner = lax.dynamic_index_in_dim(lead, (my_row ^ my_col) & (LEAD - 1), 0)
    beside = lax.dynamic_index_in_dim(lead, (my_row ^ my_col ^ 1) & (LEAD - 1), 0)
    far = swap(jnp.concatenate([corner, beside]), "row", 3)[1]
    partner = swap(lead, "row", 1)[1]
    lead = jnp.concatenate([lead, partner, swap(corner, "row", 2)[1], far])
    _, down = lax.optimization_barrier((partner, mine[:, 0]))
    down = exchange(copy_down(down, "col"), "col")
    _, across = lax.optimization_barrier((partner, across))
    across = swap(across, "row", 2)
    l_cols, k_rows = [], []
    args = [marks, lead]
    for p, (low, high) in enumerate(PARTS):
        column, row, *state = factor_columns(low, high, n, args)
        l_cols.append(column)
        k_rows.append(row)
        if high == LEAD:
            break
        if p == len(PARTS) - 2:
            state[0], *across = lax.optimization_barrier((state[0], *across))
            across = swap(jnp.stack(across), "row", 1)
        args = [state[0], jnp.concatenate(l_cols, axis=1), k_rows[0]]
    row, *moved = lax.optimization_barrier((k_rows[-1], *across, *down))
    k_rows[-1] = row
    across, down = moved[:2], jnp.stack(moved[2:])
    out = update(cols, marks, mine, down, across, (*l_cols, *k_rows))
    return out.reshape(tile_rows, 1, tile_cols, 1, n, n)


def solution(mesh):
    in_specs = (P(None, "row", None, "col", None, None), P())
    out_specs = P(None, "row", None, "col", None, None)
    return jax.shard_map(on_device, mesh=mesh, in_specs=in_specs, out_specs=out_specs, check_vma=False)
```
